32 devices in a mesh: grp: 2 (over x), lx: 4 (over y, core), ly: 4 (over z).
Axes of the slice: x: 2, y: 2, z: 4, core: 2. Of those that a mesh axis runs over, the one named last changes fastest.
Arguments:
- vectors: float32 [8, 256, 2048], P('grp', 'lx', 'ly'), may hold values from -6 to 6
- levels: int32 [256, 2048], P('lx', 'ly'), may hold values from 0 to 7
- level_table: float32 [8], replicated, may hold values from 1 to 3
- filter_low: float32 [1], replicated, may hold values from -1 to 0.5
- filter_high: float32 [1], replicated, may hold values from 6 to 7.5
Outputs:
- basis: float32 [8, 256, 2048], P('grp', 'lx', 'ly')
The draws below stay inside these ranges and needn't reach their ends.
All inputs are finite; a program needn't handle non-finite values.
Results may differ from the reference program's by a relative error of at most 0.00011.
Values sent between devices are 32-bit elements; how exact they have to be, the bound alone decides.
A program may use at most 64 MiB of HBM per device.

```python
import jax
import jax.numpy as jnp
from jax import lax

VB = 4
LEVELS = 8
NVEC = 8
NX = 256
NY = 2048
N_GRP = 2


def set_ends(array, key, least, high):
    index_at = [jax.random.randint(jax.random.fold_in(key, axis), (), 0, length) for axis, length in enumerate(array.shape)]
    main_axis = array.shape.index(max(array.shape))
    beside = index_at[:main_axis] + [(index_at[main_axis] + 1) % array.shape[main_axis]] + index_at[main_axis + 1:]
    return array.at[tuple(index_at)].set(least).at[tuple(beside)].set(high)


def block_levels(stream_key, dims, split, smallest, top_value):
    def one(axis_at, shards_of):
        heights = jax.random.uniform(jax.random.fold_in(jax.random.fold_in(stream_key, 6), axis_at), (shards_of,), jnp.float32, smallest / len(split), top_value / len(split))
        return jnp.repeat(jnp.exp(heights), dims[axis_at] // shards_of).reshape((-1,) + (1,) * (len(dims) - axis_at - 1))

    loudness = one(*split[0])
    for cut in split[1:]:
        loudness = loudness * one(*cut)
    return loudness


def scatter_about(own_key, shape, spread, reach, split=(), kind=jnp.bfloat16):
    drawn = spread * jax.random.normal(own_key, shape, jnp.float32)
    if split:
        drawn = drawn * block_levels(own_key, shape, split, -0.22, 0.18)
    return jnp.clip(drawn, -reach, reach).astype(kind)


def setup_inputs(seed: int = 0) -> dict:
    splits = jax.random.split(jax.random.key(seed), 6)
    return {
        "vectors": scatter_about(splits[0], (NVEC, NX, NY), 1.0, 6.0, ((0, 2), (1, 4), (2, 4)), jnp.float32),
        "levels": set_ends(jax.random.randint(splits[1], (NX, NY), 0, LEVELS), jax.random.fold_in(splits[1], 1), 0, LEVELS - 1).astype(jnp.int32),
        "level_table": jnp.clip(jax.random.uniform(splits[2], (LEVELS,), jnp.float32, 1.0, 3.0), 1.0, 3.0),
        "filter_low": jnp.clip(jax.random.uniform(splits[3], (1,), jnp.float32, -1.0, 0.5), -1.0, 0.5),
        "filter_high": jnp.clip(jax.random.uniform(splits[4], (1,), jnp.float32, 6.0, 7.5), 6.0, 7.5),
    }


def apply_operator(field, onsite):
    beside = jnp.roll(field, 1, 1) + jnp.roll(field, -1, 1) + jnp.roll(field, 1, 2) + jnp.roll(field, -1, 2)
    return onsite[None] * field - beside

def reference(vectors, levels, level_table, filter_low, filter_high):
    onsite = jnp.take(level_table, levels, axis=0)
    center = (filter_high[0] + filter_low[0]) / 2.0
    half = (filter_high[0] - filter_low[0]) / 2.0
    first = (apply_operator(vectors, onsite) - center * vectors) / half
    filtered = 2.0 * (apply_operator(first, onsite) - center * first) / half - vectors
    total = NX * NY
    blocks = [filtered[g * VB:(g + 1) * VB].reshape(VB, total) for g in range(N_GRP)]
    finished = []
    eye_small = jnp.eye(VB, dtype=jnp.float32)
    for h in range(N_GRP):
        current = blocks[h]
        gram = jnp.dot(current, current.T, precision=lax.Precision.HIGHEST) / total
        lower = jnp.linalg.cholesky(gram)
        inverse = lax.linalg.triangular_solve(lower, eye_small, left_side=True, lower=True)
        done = jnp.dot(inverse, current, precision=lax.Precision.HIGHEST)
        finished.append(done)
        for g in range(h + 1, N_GRP):
            coeff = jnp.dot(done, blocks[g].T, precision=lax.Precision.HIGHEST) / total
            blocks[g] = blocks[g] - jnp.dot(coeff.T, done, precision=lax.Precision.HIGHEST)
    return jnp.concatenate(finished, axis=0).reshape(NVEC, NX, NY)
```

```python
import functools

import jax
import jax.numpy as jnp
from jax import lax
from jax.experimental import pallas as pl
from jax.experimental.pallas import tpu as pltpu
from jax.sharding import PartitionSpec as P

MESH_IDS = pl.DeviceIdType.MESH
SUB, LANE = 8, 128


def padded_2(shard, sides, width):
    for axis, dim in sides:
        size, length = (lax.axis_size(axis), shard.shape[dim])
        up = [(i, (i + 1) % size) for i in range(size)]
        down = [(j, i) for i, j in up]
        last = lax.slice_in_dim(shard, length - width, length, axis=dim)
        leading = lax.slice_in_dim(shard, 0, width, axis=dim)
        before = lax.ppermute(last, axis, up)
        after = lax.ppermute(leading, axis, down)
        shard = jnp.concatenate([before, shard, after], axis=dim)
    return shard


def from_root(value, axis, source):
    kept = jnp.where(lax.axis_index(axis) == source, value, 0).astype(value.dtype)
    return lax.psum(kept, axis)


def apply_operator(field, onsite):
    padded = padded_2(field, (("lx", 1), ("ly", 2)), 1)
    beside = padded[:, 2:, 1:-1] + padded[:, :-2, 1:-1] + padded[:, 1:-1, 2:] + padded[:, 1:-1, :-2]
    return onsite[None] * field - beside


def lower_inverse(gram):
    lower = jnp.linalg.cholesky(gram)
    eye_block = jnp.eye(gram.shape[0], dtype=jnp.float32)
    return lax.linalg.triangular_solve(lower, eye_block, left_side=True, lower=True)


def general_body(vectors, levels, level_table, filter_low, filter_high):
    count_vec, rows_local, cols_local = vectors.shape
    level_ids = jnp.arange(level_table.shape[0], dtype=jnp.int32)
    onsite = jnp.sum(
        jnp.where(levels[None] == level_ids[:, None, None], level_table[:, None, None], 0.0), axis=0
    )
    center = (filter_high[0] + filter_low[0]) / 2.0
    half = (filter_high[0] - filter_low[0]) / 2.0
    first = (apply_operator(vectors, onsite) - center * vectors) / half
    filtered = 2.0 * (apply_operator(first, onsite) - center * first) / half - vectors
    total = rows_local * cols_local * lax.axis_size("lx") * lax.axis_size("ly")
    flat = filtered.reshape(count_vec, rows_local * cols_local)
    highest = lax.Precision.HIGHEST
    mine = lax.axis_index("grp")
    result = jnp.zeros_like(flat)
    for h in range(lax.axis_size("grp")):
        gram = lax.psum(jnp.dot(flat, flat.T, precision=highest), ("lx", "ly")) / total
        done = jnp.dot(lower_inverse(gram), flat, precision=highest)
        result = jnp.where(mine == h, done, result)
        shared = from_root(done, "grp", h)
        coeff = lax.psum(jnp.dot(shared, flat.T, precision=highest), ("lx", "ly")) / total
        later = mine > h
        flat = jnp.where(later, flat - jnp.dot(coeff.T, shared, precision=highest), flat)
    return result.reshape(count_vec, rows_local, cols_local)


def pair_rows(count):
    return [(i, j) for i in range(count) for j in range(i + 1)]


def lane_ids(shape):
    return lax.broadcasted_iota(jnp.int32, shape, len(shape) - 1)


def inverse_of_factor(gram, size):
    lower, inverse, recip = {}, {}, []
    for j in range(size):
        for i in range(j, size):
            value = gram[i, j]
            for k in range(j):
                value = value - lower[i, k] * lower[j, k]
            if i == j:
                recip.append(1.0 / jnp.sqrt(value))
            else:
                lower[i, j] = value * recip[j]
    for j in range(size):
        inverse[j, j] = recip[j]
        for i in range(j + 1, size):
            value = lower[i, j] * inverse[j, j]
            for k in range(j + 1, i):
                value = value + lower[i, k] * inverse[k, j]
            inverse[i, j] = -(value * recip[i])
    return inverse


def kernel(
    sizes, vec_hbm, lev_hbm, table_ref, low_ref, high_ref, out_hbm,
    field, level, onsite, filt, other, result,
    row_send, row_recv, col_send, col_recv, parts, partial, grams, factors,
    load_sem, halo_send, halo_recv, swap_send, swap_recv, gram_send, gram_recv, store_sem,
):
    n_lx, n_ly = sizes
    count, rows, cols = vec_hbm.shape
    n_levels = table_ref.shape[0]
    grp, lx, ly = lax.axis_index("grp"), lax.axis_index("lx"), lax.axis_index("ly")
    n_all = 2 * n_lx * n_ly
    me = (grp * n_lx + lx) * n_ly + ly
    r0, r1, c0, c1 = SUB, SUB + rows, LANE, LANE + cols
    half_rows = rows // 2

    def place(index):
        return (index // (n_lx * n_ly), (index // n_ly) % n_lx, index % n_ly)

    loads = [pltpu.make_async_copy(lev_hbm, level, load_sem.at[0])]
    loads += [
        pltpu.make_async_copy(vec_hbm.at[v], field.at[v, pl.ds(r0, rows), pl.ds(c0, cols)], load_sem.at[1 + v])
        for v in range(count)
    ]
    for copy in loads:
        copy.start()

    barrier = pltpu.get_barrier_semaphore()
    for d in range(1, n_all):
        pl.semaphore_signal(barrier, inc=1, device_id=place((me + d) % n_all), device_id_type=MESH_IDS)

    for copy in loads:
        copy.wait()

    lev = level[...]
    site = jnp.zeros(lev.shape, jnp.float32)
    for k in range(n_levels):
        site = jnp.where(lev == k, table_ref[k], site)
    onsite[r0:r1, c0:c1] = site
    for v in range(count):
        row_send[0, 2 * v:2 * v + 2, :] = field[v, r1 - 2:r1, c0:c1]
        row_send[1, 2 * v:2 * v + 2, :] = field[v, r0:r0 + 2, c0:c1]
    row_send[0, 2 * count:2 * count + 1, :] = onsite[r1 - 1:r1, c0:c1]
    row_send[1, 2 * count:2 * count + 1, :] = onsite[r0:r0 + 1, c0:c1]
    lanes = lane_ids((rows, LANE))
    ends = onsite[r0:r1, c1 - LANE:c1]
    begins = onsite[r0:r1, c0:c0 + LANE]
    right = pltpu.roll(ends, LANE - 2 * count, 1)
    left = pltpu.roll(begins, 2 * count, 1)
    for v in range(count):
        here = field[v, r0:r1, c1 - LANE:c1]
        here = here if v == 0 else pltpu.roll(here, LANE - 2 * v, 1)
        right = jnp.where((lanes >= LANE - 2 - 2 * v) & (lanes < LANE - 2 * v), here, right)
        here = field[v, r0:r1, c0:c0 + LANE]
        here = here if v == 0 else pltpu.roll(here, 2 * v, 1)
        left = jnp.where((lanes >= 2 * v) & (lanes < 2 * v + 2), here, left)
    col_send[0] = right
    col_send[1] = left

    pl.semaphore_wait(barrier, n_all - 1)

    up, down = (lx + n_lx - 1) % n_lx, (lx + 1) % n_lx
    west, east = (ly + n_ly - 1) % n_ly, (ly + 1) % n_ly
    halos = []

    def halo(src, dst, x, y):
        k = len(halos)
        copy = pltpu.make_async_remote_copy(
            src_ref=src, dst_ref=dst, send_sem=halo_send.at[k], recv_sem=halo_recv.at[k],
            device_id=(grp, x, y), device_id_type=MESH_IDS,
        )
        copy.start()
        halos.append(copy)

    for side, y in ((0, east), (1, west)):
        halo(col_send.at[side], col_recv.at[side, pl.ds(r0, rows)], lx, y)
        halo(col_send.at[side, pl.ds(rows - SUB, SUB)], col_recv.at[side, pl.ds(0, SUB)], down, y)
        halo(col_send.at[side, pl.ds(0, SUB)], col_recv.at[side, pl.ds(r1, SUB)], up, y)
    halo(row_send.at[0], row_recv.at[0], down, ly)
    halo(row_send.at[1], row_recv.at[1], up, ly)
    for copy in halos:
        copy.wait()

    for v in range(count):
        field[v, r0 - 2:r0, c0:c1] = row_recv[0, 2 * v:2 * v + 2, :]
        field[v, r1:r1 + 2, c0:c1] = row_recv[1, 2 * v:2 * v + 2, :]
        field[v, :, 0:LANE] = pltpu.roll(col_recv[0], 2 * v, 1) if v else col_recv[0]
        field[v, :, c1:c1 + LANE] = pltpu.roll(col_recv[1], LANE - 2 * v, 1) if v else col_recv[1]
    onsite[r0 - 1:r0, c0:c1] = row_recv[0, 2 * count:2 * count + 1, :]
    onsite[r1:r1 + 1, c0:c1] = row_recv[1, 2 * count:2 * count + 1, :]
    onsite[:, 0:LANE] = pltpu.roll(col_recv[0], 2 * count, 1)
    onsite[:, c1:c1 + LANE] = pltpu.roll(col_recv[1], LANE - 2 * count, 1)

    low = jnp.full((1, 1), low_ref[0], jnp.float32)
    high = jnp.full((1, 1), high_ref[0], jnp.float32)
    center = (high + low) * 0.5
    scale = 2.0 / (high - low)
    diagonal = (onsite[...] - center) * scale
    high_rows, wide = r1 + SUB, c1 + LANE

    def beside(x):
        return (pltpu.roll(x, 1, 0) + pltpu.roll(x, high_rows - 1, 0)
                + pltpu.roll(x, 1, 1) + pltpu.roll(x, wide - 1, 1))

    for v in range(count):
        x = field[v]
        first = diagonal * x - beside(x) * scale
        second = 2.0 * (diagonal * first - beside(first) * scale) - x
        filt[v] = second[r0:r1, c0:c1]

    away = pl.multiple_of((1 - grp) * half_rows, half_rows)
    near = pl.multiple_of(grp * half_rows, half_rows)
    swap = pltpu.make_async_remote_copy(
        src_ref=filt.at[:, pl.ds(away, half_rows)], dst_ref=other.at[:, pl.ds(away, half_rows)],
        send_sem=swap_send.at[0], recv_sem=swap_recv.at[0],
        device_id=(1 - grp, lx, ly), device_id_type=MESH_IDS,
    )
    swap.start()
    rest = pltpu.make_async_remote_copy(
        src_ref=filt.at[:, pl.ds(0, half_rows)], dst_ref=other.at[:, pl.ds(0, half_rows)],
        send_sem=swap_send.at[1], recv_sem=swap_recv.at[1],
        device_id=(1 - grp, lx, ly), device_id_type=MESH_IDS,
    )

    @pl.when(grp == 0)
    def _():
        rest.start()

    def folded(a, b):
        prod = a * b
        acc = prod[:, 0:LANE]
        for k in range(1, cols // LANE):
            acc = acc + prod[:, k * LANE:(k + 1) * LANE]
        return jnp.sum(acc, axis=0, keepdims=True)

    pairs = pair_rows(count)
    n_self, n_cross = len(pairs), count * count
    parts[...] = jnp.zeros(parts.shape, jnp.float32)
    for p, (i, j) in enumerate(pairs):
        value = folded(filt[i], filt[j])
        parts[p:p + 1, :] = jnp.where(grp == 0, value, 0.0)
        q = n_self + n_cross + p
        parts[q:q + 1, :] = jnp.where(grp == 0, 0.0, value)
    swap.wait()
    cross = {}
    for a in range(count):
        for b in range(count):
            cross[a, b] = folded(filt[a, pl.ds(near, half_rows)], other[b, pl.ds(near, half_rows)])
    for i in range(count):
        for j in range(count):
            p = n_self + i * count + j
            parts[p:p + 1, :] = jnp.where(grp == 0, cross[j, i], cross[i, j])

    depth = parts.shape[0]
    diag = lane_ids((depth, LANE)) == lax.broadcasted_iota(jnp.int32, (depth, LANE), 0)
    sums = jnp.sum(parts[...], axis=1, keepdims=True)
    packed = jnp.sum(jnp.where(diag, sums, 0.0), axis=0, keepdims=True)
    partial[0] = packed
    sends = []
    for d in range(1, n_all):
        to = (me + d) % n_all
        copy = pltpu.make_async_remote_copy(
            src_ref=partial.at[0], dst_ref=grams.at[me], send_sem=gram_send.at[d], recv_sem=gram_recv.at[me],
            device_id=place(to), device_id_type=MESH_IDS,
        )
        copy.start()
        sends.append(copy)
    grams[me] = packed
    for d in range(1, n_all):
        source = (me + d) % n_all
        pltpu.make_async_remote_copy(
            src_ref=partial.at[0], dst_ref=grams.at[source], send_sem=gram_send.at[d], recv_sem=gram_recv.at[source],
            device_id=place(source), device_id_type=MESH_IDS,
        ).wait_recv()
    total = rows * cols * n_lx * n_ly
    whole = jnp.sum(grams[...], axis=0) / total
    column = jnp.sum(jnp.where(diag, whole, 0.0), axis=1, keepdims=True)
    spread = jnp.broadcast_to(column, (depth, LANE))
    gram = {}
    for p, (i, j) in enumerate(pairs):
        gram[i, j] = spread[p:p + 1]
        q = n_self + n_cross + p
        gram[count + i, count + j] = spread[q:q + 1]
    for i in range(count):
        for j in range(count):
            p = n_self + i * count + j
            gram[count + i, j] = spread[p:p + 1]
    inverse = inverse_of_factor(gram, 2 * count)
    for (i, j), value in inverse.items():
        factors[i, j] = value

    def tiles(start):
        return [pl.ds(start + k * SUB, SUB) for k in range(half_rows // SUB)]

    def combine(start, with_other):
        for k in range(half_rows // SUB):
            at = pl.ds(start + k * SUB, SUB)
            for t in range(cols // LANE):
                on = pl.ds(t * LANE, LANE)
                own = [filt[v, at, on] for v in range(count)]
                if with_other:
                    before = [other[v, at, on] for v in range(count)]
                for i in range(count):
                    if with_other:
                        row = count + i
                        value = factors[row, count] * own[0]
                        for j in range(1, i + 1):
                            value = value + factors[row, count + j] * own[j]
                        for j in range(count):
                            value = value + factors[row, j] * before[j]
                    else:
                        value = factors[i, 0] * own[0]
                        for j in range(1, i + 1):
                            value = value + factors[i, j] * own[j]
                    result[i, at, on] = value

    stores = [
        pltpu.make_async_copy(
            result.at[:, pl.ds(s, half_rows)], out_hbm.at[:, pl.ds(s, half_rows)], store_sem.at[k]
        )
        for k, s in enumerate((half_rows, 0))
    ]

    @pl.when(grp == 0)
    def _():
        combine(half_rows, False)
        stores[0].start()
        combine(0, False)
        stores[1].start()
        rest.wait_send()

    @pl.when(grp == 1)
    def _():
        combine(half_rows, True)
        stores[0].start()
        rest.wait_recv()
        combine(0, True)
        stores[1].start()

    for copy in sends:
        copy.wait_send()
    for copy in stores:
        copy.wait()


def fused_body(sizes, vectors, levels, level_table, filter_low, filter_high):
    count, rows, cols = vectors.shape
    n_all = 2 * sizes[0] * sizes[1]
    high, wide = rows + 2 * SUB, cols + 2 * LANE
    n_pairs = count * (2 * count + 1)
    depth = -(-n_pairs // SUB) * SUB
    packed_rows = -(-(2 * count + 1) // SUB) * SUB
    f32 = jnp.float32
    smem = pl.BlockSpec(memory_space=pltpu.SMEM)
    anywhere = pl.BlockSpec(memory_space=pl.ANY)
    dma = pltpu.SemaphoreType.DMA
    return pl.pallas_call(
        functools.partial(kernel, sizes),
        out_shape=jax.ShapeDtypeStruct((count, rows, cols), f32),
        in_specs=[anywhere, anywhere, smem, smem, smem],
        out_specs=anywhere,
        scratch_shapes=[
            pltpu.VMEM((count, high, wide), f32),
            pltpu.VMEM((rows, cols), jnp.int32),
            pltpu.VMEM((high, wide), f32),
            pltpu.VMEM((count, rows, cols), f32),
            pltpu.VMEM((count, rows, cols), f32),
            pltpu.VMEM((count, rows, cols), f32),
            pltpu.VMEM((2, packed_rows, cols), f32),
            pltpu.VMEM((2, packed_rows, cols), f32),
            pltpu.VMEM((2, rows, LANE), f32),
            pltpu.VMEM((2, high, LANE), f32),
            pltpu.VMEM((depth, LANE), f32),
            pltpu.VMEM((1, 1, LANE), f32),
            pltpu.VMEM((n_all, 1, LANE), f32),
            pltpu.VMEM((2 * count, 2 * count, 1, LANE), f32),
            dma((1 + count,)),
            dma((8,)),
            dma((8,)),
            dma((2,)),
            dma((2,)),
            dma((n_all,)),
            dma((n_all,)),
            dma((2,)),
        ],
        compiler_params=pltpu.CompilerParams(
            collective_id=0, has_side_effects=True, vmem_limit_bytes=32 * 1024 * 1024
        ),
    )(vectors, levels, level_table, filter_low, filter_high)


def solution(mesh):
    in_specs = (P("grp", "lx", "ly"), P("lx", "ly"), P(), P(), P())
    out_specs = P("grp", "lx", "ly")
    if mesh.shape["grp"] == 2:
        body = functools.partial(fused_body, (mesh.shape["lx"], mesh.shape["ly"]))
    else:
        body = general_body
    return jax.shard_map(body, mesh=mesh, in_specs=in_specs, out_specs=out_specs, check_vma=False)
```

```python
import functools

import jax
import jax.numpy as jnp
from jax import lax
from jax.experimental import pallas as pl
from jax.experimental.pallas import tpu as pltpu
from jax.sharding import PartitionSpec as P

MESH_IDS = pl.DeviceIdType.MESH
SUB, LANE = 8, 128


def padded_2(shard, sides, width):
    for axis, dim in sides:
        size, length = (lax.axis_size(axis), shard.shape[dim])
        up = [(i, (i + 1) % size) for i in range(size)]
        down = [(j, i) for i, j in up]
        last = lax.slice_in_dim(shard, length - width, length, axis=dim)
        leading = lax.slice_in_dim(shard, 0, width, axis=dim)
        before = lax.ppermute(last, axis, up)
        after = lax.ppermute(leading, axis, down)
        shard = jnp.concatenate([before, shard, after], axis=dim)
    return shard


def from_root(value, axis, source):
    kept = jnp.where(lax.axis_index(axis) == source, value, 0).astype(value.dtype)
    return lax.psum(kept, axis)


def apply_operator(field, onsite):
    padded = padded_2(field, (("lx", 1), ("ly", 2)), 1)
    beside = padded[:, 2:, 1:-1] + padded[:, :-2, 1:-1] + padded[:, 1:-1, 2:] + padded[:, 1:-1, :-2]
    return onsite[None] * field - beside


def lower_inverse(gram):
    lower = jnp.linalg.cholesky(gram)
    eye_block = jnp.eye(gram.shape[0], dtype=jnp.float32)
    return lax.linalg.triangular_solve(lower, eye_block, left_side=True, lower=True)


def general_body(vectors, levels, level_table, filter_low, filter_high):
    count_vec, rows_local, cols_local = vectors.shape
    level_ids = jnp.arange(level_table.shape[0], dtype=jnp.int32)
    onsite = jnp.sum(
        jnp.where(levels[None] == level_ids[:, None, None], level_table[:, None, None], 0.0), axis=0
    )
    center = (filter_high[0] + filter_low[0]) / 2.0
    half = (filter_high[0] - filter_low[0]) / 2.0
    first = (apply_operator(vectors, onsite) - center * vectors) / half
    filtered = 2.0 * (apply_operator(first, onsite) - center * first) / half - vectors
    total = rows_local * cols_local * lax.axis_size("lx") * lax.axis_size("ly")
    flat = filtered.reshape(count_vec, rows_local * cols_local)
    highest = lax.Precision.HIGHEST
    mine = lax.axis_index("grp")
    result = jnp.zeros_like(flat)
    for h in range(lax.axis_size("grp")):
        gram = lax.psum(jnp.dot(flat, flat.T, precision=highest), ("lx", "ly")) / total
        done = jnp.dot(lower_inverse(gram), flat, precision=highest)
        result = jnp.where(mine == h, done, result)
        shared = from_root(done, "grp", h)
        coeff = lax.psum(jnp.dot(shared, flat.T, precision=highest), ("lx", "ly")) / total
        later = mine > h
        flat = jnp.where(later, flat - jnp.dot(coeff.T, shared, precision=highest), flat)
    return result.reshape(count_vec, rows_local, cols_local)


def pair_rows(count):
    return [(i, j) for i in range(count) for j in range(i + 1)]


def lane_ids(shape):
    return lax.broadcasted_iota(jnp.int32, shape, len(shape) - 1)


def inverse_of_factor(gram, size):
    lower, inverse, recip = {}, {}, []
    for j in range(size):
        for i in range(j, size):
            value = gram[i, j]
            for k in range(j):
                value = value - lower[i, k] * lower[j, k]
            if i == j:
                recip.append(1.0 / jnp.sqrt(value))
            else:
                lower[i, j] = value * recip[j]
    for j in range(size):
        inverse[j, j] = recip[j]
        for i in range(j + 1, size):
            value = lower[i, j] * inverse[j, j]
            for k in range(j + 1, i):
                value = value + lower[i, k] * inverse[k, j]
            inverse[i, j] = -(value * recip[i])
    return inverse


def kernel(
    sizes, vec_hbm, lev_hbm, table_hbm, low_hbm, high_hbm, out_hbm,
    table_ref, low_ref, high_ref, field, level, onsite, filt, other, result,
    row_send, row_recv, col_send, col_recv, parts, partial, grams, factors,
    load_sem, halo_send, halo_recv, swap_send, swap_recv, gram_send, gram_recv, store_sem,
):
    n_lx, n_ly = sizes
    count, rows, cols = vec_hbm.shape
    n_levels = table_ref.shape[0]
    grp, lx, ly = lax.axis_index("grp"), lax.axis_index("lx"), lax.axis_index("ly")
    n_all = 2 * n_lx * n_ly
    me = (grp * n_lx + lx) * n_ly + ly
    r0, r1, c0, c1 = SUB, SUB + rows, LANE, LANE + cols
    half_rows = rows // 2

    def place(index):
        return (index // (n_lx * n_ly), (index // n_ly) % n_lx, index % n_ly)

    loads = [pltpu.make_async_copy(lev_hbm, level, load_sem.at[0])]
    loads += [
        pltpu.make_async_copy(src, dst, load_sem.at[1 + count + k])
        for k, (src, dst) in enumerate(((table_hbm, table_ref), (low_hbm, low_ref), (high_hbm, high_ref)))
    ]
    loads += [
        pltpu.make_async_copy(vec_hbm.at[v], field.at[v, pl.ds(r0, rows), pl.ds(c0, cols)], load_sem.at[1 + v])
        for v in range(count)
    ]
    for copy in loads:
        copy.start()

    barrier = pltpu.get_barrier_semaphore()
    for d in range(1, n_all):
        pl.semaphore_signal(barrier, inc=1, device_id=place((me + d) % n_all), device_id_type=MESH_IDS)

    for copy in loads:
        copy.wait()

    lev = level[...]
    site = jnp.zeros(lev.shape, jnp.float32)
    for k in range(n_levels):
        site = jnp.where(lev == k, table_ref[k], site)
    onsite[r0:r1, c0:c1] = site
    for v in range(count):
        row_send[0, 2 * v:2 * v + 2, :] = field[v, r1 - 2:r1, c0:c1]
        row_send[1, 2 * v:2 * v + 2, :] = field[v, r0:r0 + 2, c0:c1]
    row_send[0, 2 * count:2 * count + 1, :] = onsite[r1 - 1:r1, c0:c1]
    row_send[1, 2 * count:2 * count + 1, :] = onsite[r0:r0 + 1, c0:c1]
    lanes = lane_ids((rows, LANE))
    ends = onsite[r0:r1, c1 - LANE:c1]
    begins = onsite[r0:r1, c0:c0 + LANE]
    right = pltpu.roll(ends, LANE - 2 * count, 1)
    left = pltpu.roll(begins, 2 * count, 1)
    for v in range(count):
        here = field[v, r0:r1, c1 - LANE:c1]
        here = here if v == 0 else pltpu.roll(here, LANE - 2 * v, 1)
        right = jnp.where((lanes >= LANE - 2 - 2 * v) & (lanes < LANE - 2 * v), here, right)
        here = field[v, r0:r1, c0:c0 + LANE]
        here = here if v == 0 else pltpu.roll(here, 2 * v, 1)
        left = jnp.where((lanes >= 2 * v) & (lanes < 2 * v + 2), here, left)
    col_send[0] = right
    col_send[1] = left

    pl.semaphore_wait(barrier, n_all - 1)

    up, down = (lx + n_lx - 1) % n_lx, (lx + 1) % n_lx
    west, east = (ly + n_ly - 1) % n_ly, (ly + 1) % n_ly
    halos = []

    def halo(src, dst, x, y):
        k = len(halos)
        copy = pltpu.make_async_remote_copy(
            src_ref=src, dst_ref=dst, send_sem=halo_send.at[k], recv_sem=halo_recv.at[k],
            device_id=(grp, x, y), device_id_type=MESH_IDS,
        )
        copy.start()
        halos.append(copy)

    for side, y in ((0, east), (1, west)):
        halo(col_send.at[side], col_recv.at[side, pl.ds(r0, rows)], lx, y)
        halo(col_send.at[side, pl.ds(rows - SUB, SUB)], col_recv.at[side, pl.ds(0, SUB)], down, y)
        halo(col_send.at[side, pl.ds(0, SUB)], col_recv.at[side, pl.ds(r1, SUB)], up, y)
    halo(row_send.at[0], row_recv.at[0], down, ly)
    halo(row_send.at[1], row_recv.at[1], up, ly)
    for copy in halos:
        copy.wait()

    for v in range(count):
        field[v, r0 - 2:r0, c0:c1] = row_recv[0, 2 * v:2 * v + 2, :]
        field[v, r1:r1 + 2, c0:c1] = row_recv[1, 2 * v:2 * v + 2, :]
        field[v, :, 0:LANE] = pltpu.roll(col_recv[0], 2 * v, 1) if v else col_recv[0]
        field[v, :, c1:c1 + LANE] = pltpu.roll(col_recv[1], LANE - 2 * v, 1) if v else col_recv[1]
    onsite[r0 - 1:r0, c0:c1] = row_recv[0, 2 * count:2 * count + 1, :]
    onsite[r1:r1 + 1, c0:c1] = row_recv[1, 2 * count:2 * count + 1, :]
    onsite[:, 0:LANE] = pltpu.roll(col_recv[0], 2 * count, 1)
    onsite[:, c1:c1 + LANE] = pltpu.roll(col_recv[1], LANE - 2 * count, 1)

    low = jnp.full((1, 1), low_ref[0], jnp.float32)
    high = jnp.full((1, 1), high_ref[0], jnp.float32)
    center = (high + low) * 0.5
    scale = 2.0 / (high - low)
    diagonal = (onsite[...] - center) * scale
    high_rows, wide = r1 + SUB, c1 + LANE

    def beside(x):
        return (pltpu.roll(x, 1, 0) + pltpu.roll(x, high_rows - 1, 0)
                + pltpu.roll(x, 1, 1) + pltpu.roll(x, wide - 1, 1))

    for v in range(count):
        x = field[v]
        first = diagonal * x - beside(x) * scale
        second = 2.0 * (diagonal * first - beside(first) * scale) - x
        filt[v] = second[r0:r1, c0:c1]

    away = pl.multiple_of((1 - grp) * half_rows, half_rows)
    near = pl.multiple_of(grp * half_rows, half_rows)
    swap = pltpu.make_async_remote_copy(
        src_ref=filt.at[:, pl.ds(away, half_rows)], dst_ref=other.at[:, pl.ds(away, half_rows)],
        send_sem=swap_send.at[0], recv_sem=swap_recv.at[0],
        device_id=(1 - grp, lx, ly), device_id_type=MESH_IDS,
    )
    swap.start()
    rest = pltpu.make_async_remote_copy(
        src_ref=filt.at[:, pl.ds(0, half_rows)], dst_ref=other.at[:, pl.ds(0, half_rows)],
        send_sem=swap_send.at[1], recv_sem=swap_recv.at[1],
        device_id=(1 - grp, lx, ly), device_id_type=MESH_IDS,
    )

    @pl.when(grp == 0)
    def _():
        rest.start()

    def folded(a, b):
        prod = a * b
        acc = prod[:, 0:LANE]
        for k in range(1, cols // LANE):
            acc = acc + prod[:, k * LANE:(k + 1) * LANE]
        return jnp.sum(acc, axis=0, keepdims=True)

    pairs = pair_rows(count)
    n_self, n_cross = len(pairs), count * count
    parts[...] = jnp.zeros(parts.shape, jnp.float32)
    for p, (i, j) in enumerate(pairs):
        value = folded(filt[i], filt[j])
        parts[p:p + 1, :] = jnp.where(grp == 0, value, 0.0)
        q = n_self + n_cross + p
        parts[q:q + 1, :] = jnp.where(grp == 0, 0.0, value)
    swap.wait()
    cross = {}
    for a in range(count):
        for b in range(count):
            cross[a, b] = folded(filt[a, pl.ds(near, half_rows)], other[b, pl.ds(near, half_rows)])
    for i in range(count):
        for j in range(count):
            p = n_self + i * count + j
            parts[p:p + 1, :] = jnp.where(grp == 0, cross[j, i], cross[i, j])

    depth = parts.shape[0]
    diag = lane_ids((depth, LANE)) == lax.broadcasted_iota(jnp.int32, (depth, LANE), 0)
    sums = jnp.sum(parts[...], axis=1, keepdims=True)
    packed = jnp.sum(jnp.where(diag, sums, 0.0), axis=0, keepdims=True)
    partial[0] = packed
    sends = []
    for d in range(1, n_all):
        to = (me + d) % n_all
        copy = pltpu.make_async_remote_copy(
            src_ref=partial.at[0], dst_ref=grams.at[me], send_sem=gram_send.at[d], recv_sem=gram_recv.at[me],
            device_id=place(to), device_id_type=MESH_IDS,
        )
        copy.start()
        sends.append(copy)
    grams[me] = packed
    for d in range(1, n_all):
        source = (me + d) % n_all
        pltpu.make_async_remote_copy(
            src_ref=partial.at[0], dst_ref=grams.at[source], send_sem=gram_send.at[d], recv_sem=gram_recv.at[source],
            device_id=place(source), device_id_type=MESH_IDS,
        ).wait_recv()
    total = rows * cols * n_lx * n_ly
    whole = jnp.sum(grams[...], axis=0) / total
    column = jnp.sum(jnp.where(diag, whole, 0.0), axis=1, keepdims=True)
    spread = jnp.broadcast_to(column, (depth, LANE))
    gram = {}
    for p, (i, j) in enumerate(pairs):
        gram[i, j] = spread[p:p + 1]
        q = n_self + n_cross + p
        gram[count + i, count + j] = spread[q:q + 1]
    for i in range(count):
        for j in range(count):
            p = n_self + i * count + j
            gram[count + i, j] = spread[p:p + 1]
    inverse = inverse_of_factor(gram, 2 * count)
    for (i, j), value in inverse.items():
        factors[i, j] = value

    def tiles(start):
        return [pl.ds(start + k * SUB, SUB) for k in range(half_rows // SUB)]

    def combine(start, with_other):
        for k in range(half_rows // SUB):
            at = pl.ds(start + k * SUB, SUB)
            for t in range(cols // LANE):
                on = pl.ds(t * LANE, LANE)
                own = [filt[v, at, on] for v in range(count)]
                if with_other:
                    before = [other[v, at, on] for v in range(count)]
                for i in range(count):
                    if with_other:
                        row = count + i
                        value = factors[row, count] * own[0]
                        for j in range(1, i + 1):
                            value = value + factors[row, count + j] * own[j]
                        for j in range(count):
                            value = value + factors[row, j] * before[j]
                    else:
                        value = factors[i, 0] * own[0]
                        for j in range(1, i + 1):
                            value = value + factors[i, j] * own[j]
                    result[i, at, on] = value

    stores = [
        pltpu.make_async_copy(
            result.at[:, pl.ds(s, half_rows)], out_hbm.at[:, pl.ds(s, half_rows)], store_sem.at[k]
        )
        for k, s in enumerate((half_rows, 0))
    ]

    @pl.when(grp == 0)
    def _():
        combine(half_rows, False)
        stores[0].start()
        combine(0, False)
        stores[1].start()
        rest.wait_send()

    @pl.when(grp == 1)
    def _():
        combine(half_rows, True)
        stores[0].start()
        rest.wait_recv()
        combine(0, True)
        stores[1].start()

    for copy in sends:
        copy.wait_send()
    for copy in stores:
        copy.wait()


def fused_body(sizes, vectors, levels, level_table, filter_low, filter_high):
    count, rows, cols = vectors.shape
    n_all = 2 * sizes[0] * sizes[1]
    high, wide = rows + 2 * SUB, cols + 2 * LANE
    n_pairs = count * (2 * count + 1)
    depth = -(-n_pairs // SUB) * SUB
    packed_rows = -(-(2 * count + 1) // SUB) * SUB
    f32 = jnp.float32
    anywhere = pl.BlockSpec(memory_space=pl.ANY)
    dma = pltpu.SemaphoreType.DMA
    return pl.pallas_call(
        functools.partial(kernel, sizes),
        out_shape=jax.ShapeDtypeStruct((count, rows, cols), f32),
        in_specs=[anywhere] * 5,
        out_specs=anywhere,
        scratch_shapes=[
            pltpu.SMEM(level_table.shape, f32),
            pltpu.SMEM(filter_low.shape, f32),
            pltpu.SMEM(filter_high.shape, f32),
            pltpu.VMEM((count, high, wide), f32),
            pltpu.VMEM((rows, cols), jnp.int32),
            pltpu.VMEM((high, wide), f32),
            pltpu.VMEM((count, rows, cols), f32),
            pltpu.VMEM((count, rows, cols), f32),
            pltpu.VMEM((count, rows, cols), f32),
            pltpu.VMEM((2, packed_rows, cols), f32),
            pltpu.VMEM((2, packed_rows, cols), f32),
            pltpu.VMEM((2, rows, LANE), f32),
            pltpu.VMEM((2, high, LANE), f32),
            pltpu.VMEM((depth, LANE), f32),
            pltpu.VMEM((1, 1, LANE), f32),
            pltpu.VMEM((n_all, 1, LANE), f32),
            pltpu.VMEM((2 * count, 2 * count, 1, LANE), f32),
            dma((4 + count,)),
            dma((8,)),
            dma((8,)),
            dma((2,)),
            dma((2,)),
            dma((n_all,)),
            dma((n_all,)),
            dma((2,)),
        ],
        compiler_params=pltpu.CompilerParams(
            collective_id=0, has_side_effects=True, vmem_limit_bytes=60 * 1024 * 1024
        ),
    )(vectors, levels, level_table, filter_low, filter_high)


def solution(mesh):
    in_specs = (P("grp", "lx", "ly"), P("lx", "ly"), P(), P(), P())
    out_specs = P("grp", "lx", "ly")
    if mesh.shape["grp"] == 2:
        body = functools.partial(fused_body, (mesh.shape["lx"], mesh.shape["ly"]))
    else:
        body = general_body
    return jax.shard_map(body, mesh=mesh, in_specs=in_specs, out_specs=out_specs, check_vma=False)
```

```python
import functools

import jax
import jax.numpy as jnp
from jax import lax
from jax.experimental import pallas as pl
from jax.experimental.pallas import tpu as pltpu
from jax.sharding import PartitionSpec as P

MESH_IDS = pl.DeviceIdType.MESH
SUB, LANE = 8, 128


def padded_2(shard, sides, width):
    for axis, dim in sides:
        size, length = (lax.axis_size(axis), shard.shape[dim])
        up = [(i, (i + 1) % size) for i in range(size)]
        down = [(j, i) for i, j in up]
        last = lax.slice_in_dim(shard, length - width, length, axis=dim)
        leading = lax.slice_in_dim(shard, 0, width, axis=dim)
        before = lax.ppermute(last, axis, up)
        after = lax.ppermute(leading, axis, down)
        shard = jnp.concatenate([before, shard, after], axis=dim)
    return shard


def from_root(value, axis, source):
    kept = jnp.where(lax.axis_index(axis) == source, value, 0).astype(value.dtype)
    return lax.psum(kept, axis)


def apply_operator(field, onsite):
    padded = padded_2(field, (("lx", 1), ("ly", 2)), 1)
    beside = padded[:, 2:, 1:-1] + padded[:, :-2, 1:-1] + padded[:, 1:-1, 2:] + padded[:, 1:-1, :-2]
    return onsite[None] * field - beside


def lower_inverse(gram):
    lower = jnp.linalg.cholesky(gram)
    eye_block = jnp.eye(gram.shape[0], dtype=jnp.float32)
    return lax.linalg.triangular_solve(lower, eye_block, left_side=True, lower=True)


def general_body(vectors, levels, level_table, filter_low, filter_high):
    count_vec, rows_local, cols_local = vectors.shape
    level_ids = jnp.arange(level_table.shape[0], dtype=jnp.int32)
    onsite = jnp.sum(
        jnp.where(levels[None] == level_ids[:, None, None], level_table[:, None, None], 0.0), axis=0
    )
    center = (filter_high[0] + filter_low[0]) / 2.0
    half = (filter_high[0] - filter_low[0]) / 2.0
    first = (apply_operator(vectors, onsite) - center * vectors) / half
    filtered = 2.0 * (apply_operator(first, onsite) - center * first) / half - vectors
    total = rows_local * cols_local * lax.axis_size("lx") * lax.axis_size("ly")
    flat = filtered.reshape(count_vec, rows_local * cols_local)
    highest = lax.Precision.HIGHEST
    mine = lax.axis_index("grp")
    result = jnp.zeros_like(flat)
    for h in range(lax.axis_size("grp")):
        gram = lax.psum(jnp.dot(flat, flat.T, precision=highest), ("lx", "ly")) / total
        done = jnp.dot(lower_inverse(gram), flat, precision=highest)
        result = jnp.where(mine == h, done, result)
        shared = from_root(done, "grp", h)
        coeff = lax.psum(jnp.dot(shared, flat.T, precision=highest), ("lx", "ly")) / total
        later = mine > h
        flat = jnp.where(later, flat - jnp.dot(coeff.T, shared, precision=highest), flat)
    return result.reshape(count_vec, rows_local, cols_local)


def pair_rows(count):
    return [(i, j) for i in range(count) for j in range(i + 1)]


def lane_ids(shape):
    return lax.broadcasted_iota(jnp.int32, shape, len(shape) - 1)


def inverse_of_factor(gram, size):
    lower, inverse, recip = {}, {}, []
    for j in range(size):
        for i in range(j, size):
            value = gram[i, j]
            for k in range(j):
                value = value - lower[i, k] * lower[j, k]
            if i == j:
                recip.append(1.0 / jnp.sqrt(value))
            else:
                lower[i, j] = value * recip[j]
    for j in range(size):
        inverse[j, j] = recip[j]
        for i in range(j + 1, size):
            value = lower[i, j] * inverse[j, j]
            for k in range(j + 1, i):
                value = value + lower[i, k] * inverse[k, j]
            inverse[i, j] = -(value * recip[i])
    return inverse


def kernel(
    sizes, vec_hbm, lev_hbm, table_hbm, low_ref, high_ref, out_hbm,
    table_ref, field, level, onsite, filt, mate, other, result,
    row_send, row_recv, col_send, col_recv, fold, mate_rows, mate_fold, mate_cols,
    parts, partial, early, grams, factors,
    load_sem, halo_send, halo_recv, grp_send, grp_recv, early_send, early_recv, gram_send, gram_recv, store_sem,
):
    n_lx, n_ly = sizes
    count, rows, cols = vec_hbm.shape
    n_levels = table_hbm.shape[0]
    grp, lx, ly = lax.axis_index("grp"), lax.axis_index("lx"), lax.axis_index("ly")
    n_plane = n_lx * n_ly
    spot = lx * n_ly + ly
    me = grp * n_plane + spot
    r0, r1, c0, c1 = SUB, SUB + rows, LANE, LANE + cols
    high, wide = r1 + SUB, c1 + LANE
    split = rows * 3 // 8 // SUB * SUB

    def place(block, index):
        index = index % n_plane
        return (block, index // n_ly, index % n_ly)

    def remote(src, dst, send, recv, to):
        return pltpu.make_async_remote_copy(
            src_ref=src, dst_ref=dst, send_sem=send, recv_sem=recv, device_id=to, device_id_type=MESH_IDS
        )

    loads = [pltpu.make_async_copy(lev_hbm, level, load_sem.at[0])]
    loads += [pltpu.make_async_copy(table_hbm, table_ref, load_sem.at[1])]
    loads += [
        pltpu.make_async_copy(vec_hbm.at[v], field.at[v, pl.ds(r0, rows), pl.ds(c0, cols)], load_sem.at[2 + v])
        for v in range(count)
    ]
    for copy in loads:
        copy.start()

    barrier = pltpu.get_barrier_semaphore()
    for d in range(1, n_plane):
        pl.semaphore_signal(barrier, inc=1, device_id=place(grp, spot + d), device_id_type=MESH_IDS)
    pl.semaphore_signal(barrier, inc=1, device_id=(1 - grp, lx, ly), device_id_type=MESH_IDS)

    @pl.when(grp == 1)
    def _():
        for d in range(1, n_plane):
            pl.semaphore_signal(barrier, inc=1, device_id=place(0, spot + d), device_id_type=MESH_IDS)

    for copy in loads:
        copy.wait()

    lev = level[...]
    site = jnp.zeros(lev.shape, jnp.float32)
    for k in range(n_levels):
        site = jnp.where(lev == k, table_ref[k], site)
    onsite[r0:r1, c0:c1] = site
    for v in range(count):
        row_send[0, 2 * v:2 * v + 2, :] = field[v, r1 - 2:r1, c0:c1]
        row_send[1, 2 * v:2 * v + 2, :] = field[v, r0:r0 + 2, c0:c1]
    row_send[0, 2 * count:2 * count + 1, :] = onsite[r1 - 1:r1, c0:c1]
    row_send[1, 2 * count:2 * count + 1, :] = onsite[r0:r0 + 1, c0:c1]
    lanes = lane_ids((rows, LANE))
    ends = onsite[r0:r1, c1 - LANE:c1]
    begins = onsite[r0:r1, c0:c0 + LANE]
    right = pltpu.roll(ends, LANE - 2 * count, 1)
    left = pltpu.roll(begins, 2 * count, 1)
    for v in range(count):
        here = field[v, r0:r1, c1 - LANE:c1]
        here = here if v == 0 else pltpu.roll(here, LANE - 2 * v, 1)
        right = jnp.where((lanes >= LANE - 2 - 2 * v) & (lanes < LANE - 2 * v), here, right)
        here = field[v, r0:r1, c0:c0 + LANE]
        here = here if v == 0 else pltpu.roll(here, 2 * v, 1)
        left = jnp.where((lanes >= 2 * v) & (lanes < 2 * v + 2), here, left)
    col_send[0] = right
    col_send[1] = left

    @pl.when(grp == 0)
    def _():
        pl.semaphore_wait(barrier, 2 * n_plane - 1)

    @pl.when(grp == 1)
    def _():
        pl.semaphore_wait(barrier, n_plane)

    up, down = (lx + n_lx - 1) % n_lx, (lx + 1) % n_lx
    west, east = (ly + n_ly - 1) % n_ly, (ly + 1) % n_ly
    halos = []

    def halo(src, dst, x, y):
        k = len(halos)
        copy = remote(src, dst, halo_send.at[k], halo_recv.at[k], (grp, x, y))
        copy.start()
        halos.append(copy)

    for side, y in ((0, east), (1, west)):
        halo(col_send.at[side], col_recv.at[side, pl.ds(r0, rows)], lx, y)
        halo(col_send.at[side, pl.ds(rows - SUB, SUB)], col_recv.at[side, pl.ds(0, SUB)], down, y)
        halo(col_send.at[side, pl.ds(0, SUB)], col_recv.at[side, pl.ds(r1, SUB)], up, y)
    halo(row_send.at[0], row_recv.at[0], down, ly)
    halo(row_send.at[1], row_recv.at[1], up, ly)

    partner = (1 - grp, lx, ly)
    n_link = [0]

    def across(src, dst):
        k = n_link[0]
        n_link[0] += 1
        return remote(src, dst, grp_send.at[k], grp_recv.at[k], partner)

    def band(start, stop):
        at = (slice(None), pl.ds(r0 + start, stop - start), pl.ds(c0, cols))
        return across(field.at[at], mate.at[at])

    lower = band(split - SUB, rows)
    upper = band(0, split - SUB)
    edges = [across(row_recv.at[k, pl.ds(0, 2 * count)], mate_rows.at[k]) for k in range(2)]
    edges.append(across(fold, mate_fold))
    back = across(filt.at[:, pl.ds(0, split)], other.at[:, pl.ds(0, split)])

    @pl.when(grp == 0)
    def _():
        lower.start()

    for copy in halos:
        copy.wait()

    group = 4 * count
    per_tile = LANE // group
    tile_lanes = lane_ids((SUB, LANE))

    @pl.when(grp == 0)
    def _():
        for t in range(fold.shape[0] // SUB):
            value = jnp.zeros((SUB, LANE), jnp.float32)
            for g in range(per_tile):
                at = (t * per_tile + g) * SUB
                if at >= high:
                    break
                both = jnp.where(tile_lanes < LANE // 2, col_recv[1, at:at + SUB], col_recv[0, at:at + SUB])
                both = pltpu.roll(both, 2 * count + group * g, 1)
                value = jnp.where((tile_lanes >= group * g) & (tile_lanes < group * (g + 1)), both, value)
            fold[t * SUB:(t + 1) * SUB] = value
        for copy in edges:
            copy.start()
        upper.start()

    def place_edges(dst, first_rows, last_rows, before, after):
        for v in range(count):
            dst[v, r0 - 2:r0, c0:c1] = first_rows[2 * v:2 * v + 2, :]
            dst[v, r1:r1 + 2, c0:c1] = last_rows[2 * v:2 * v + 2, :]
            dst[v, :, 0:LANE] = pltpu.roll(before[...], 2 * v, 1) if v else before[...]
            dst[v, :, c1:c1 + LANE] = pltpu.roll(after[...], LANE - 2 * v, 1) if v else after[...]

    place_edges(field, row_recv.at[0], row_recv.at[1], col_recv.at[0], col_recv.at[1])
    low = jnp.full((1, 1), low_ref[0], jnp.float32)
    top = jnp.full((1, 1), high_ref[0], jnp.float32)
    center = (top + low) * 0.5
    scale = 2.0 / (top - low)
    onsite[r0 - 1:r0, c0:c1] = row_recv[0, 2 * count:2 * count + 1, :]
    onsite[r1:r1 + 1, c0:c1] = row_recv[1, 2 * count:2 * count + 1, :]
    onsite[:, 0:LANE] = pltpu.roll(col_recv[0], 2 * count, 1)
    onsite[:, c1:c1 + LANE] = pltpu.roll(col_recv[1], LANE - 2 * count, 1)
    onsite[...] = (onsite[...] - center) * scale

    def filter_rows(src, dst, start, stop):
        at = pl.ds(start, stop - start + 2 * SUB)
        n = stop - start + 2 * SUB
        diagonal = onsite[at, :]

        def beside(x):
            return (pltpu.roll(x, 1, 0) + pltpu.roll(x, n - 1, 0)
                    + pltpu.roll(x, 1, 1) + pltpu.roll(x, wide - 1, 1))

        for v in range(count):
            x = src[v, at, :]
            first = diagonal * x - beside(x) * scale
            second = 2.0 * (diagonal * first - beside(first) * scale) - x
            dst[v, start:stop] = second[SUB:SUB + stop - start, c0:c1]

    filter_rows(field, filt, 0, rows)

    @pl.when(grp == 1)
    def _():
        back.start()

    pairs = pair_rows(count)
    n_self, n_cross = len(pairs), count * count
    depth = parts.shape[0]
    diag = lane_ids((depth, LANE)) == lax.broadcasted_iota(jnp.int32, (depth, LANE), 0)
    total = rows * cols * n_lx * n_ly

    def folded(a, b):
        prod = a * b
        acc = prod[:, 0:LANE]
        for k in range(1, cols // LANE):
            acc = acc + prod[:, k * LANE:(k + 1) * LANE]
        return jnp.sum(acc, axis=0, keepdims=True)

    def packed_parts():
        sums = jnp.sum(parts[...], axis=1, keepdims=True)
        return jnp.sum(jnp.where(diag, sums, 0.0), axis=0, keepdims=True)

    def spread_out(slots):
        whole = jnp.sum(slots[...], axis=0) / total
        column = jnp.sum(jnp.where(diag, whole, 0.0), axis=1, keepdims=True)
        return jnp.broadcast_to(column, (depth, LANE))

    def keep_factor(gram, size):
        for (i, j), value in inverse_of_factor(gram, size).items():
            factors[i, j] = value

    parts[...] = jnp.zeros(parts.shape, jnp.float32)
    for p, (i, j) in enumerate(pairs):
        value = folded(filt[i], filt[j])
        parts[p:p + 1, :] = jnp.where(grp == 0, value, 0.0)
        q = n_self + n_cross + p
        parts[q:q + 1, :] = jnp.where(grp == 0, 0.0, value)

    def cross_parts(block_0, block_1, start, stop):
        for i in range(count):
            for j in range(count):
                p = n_self + i * count + j
                parts[p:p + 1, :] = folded(block_1[i, start:stop], block_0[j, start:stop])

    def combine(start, stop, first_row, blocks):
        for at_row in range(start, stop, SUB):
            at = pl.ds(at_row, SUB)
            for t in range(cols // LANE):
                on = pl.ds(t * LANE, LANE)
                tiles = [block[v, at, on] for block in blocks for v in range(count)]
                for i in range(count):
                    row = first_row + i
                    value = factors[row, 0] * tiles[0]
                    for j in range(1, row + 1):
                        value = value + factors[row, j] * tiles[j]
                    result[i, at, on] = value

    middle = rows // 2 // SUB * SUB
    halves = ((0, middle), (middle, rows))
    stores = [
        pltpu.make_async_copy(result.at[:, pl.ds(s, e - s)], out_hbm.at[:, pl.ds(s, e - s)], store_sem.at[k])
        for k, (s, e) in enumerate(halves)
    ]

    def finish(first_row, blocks):
        for store, (s, e) in zip(stores, halves):
            combine(s, e, first_row, blocks)
            store.start()

    @pl.when(grp == 0)
    def _():
        partial[0] = packed_parts()
        early[spot] = partial[0]
        sends = []
        for d in range(1, n_plane):
            copy = remote(partial.at[0], early.at[spot], early_send.at[d], early_recv.at[spot], place(0, spot + d))
            copy.start()
            sends.append(copy)
        for d in range(1, n_plane):
            source = (spot + d) % n_plane
            remote(partial.at[0], early.at[source], early_send.at[d], early_recv.at[source], place(0, source)).wait_recv()
        spread = spread_out(early)
        keep_factor({(i, j): spread[p:p + 1] for p, (i, j) in enumerate(pairs)}, count)
        finish(0, [filt])
        back.wait_recv()
        cross_parts(filt, other, 0, split)
        partial[1] = packed_parts()
        for d in range(n_plane):
            copy = remote(partial.at[1], grams.at[me], gram_send.at[d], gram_recv.at[me], place(1, spot + d))
            copy.start()
            sends.append(copy)
        for copy in [lower, upper] + edges + sends:
            copy.wait_send()

    @pl.when(grp == 1)
    def _():
        for copy in edges:
            copy.wait_recv()
        for k in range(high // SUB):
            t, g = k // per_tile, k % per_tile
            tile = mate_fold[t * SUB:(t + 1) * SUB]
            mate_cols[k * SUB:(k + 1) * SUB] = pltpu.roll(tile, LANE - 2 * count - group * g, 1)
        place_edges(mate, mate_rows.at[0], mate_rows.at[1], mate_cols, mate_cols)
        lower.wait_recv()
        filter_rows(mate, other, split, rows)
        cross_parts(other, filt, split, rows)
        partial[1] = packed_parts()
        grams[me] = partial[1]
        sends = []
        for d in range(1, n_plane):
            copy = remote(partial.at[1], grams.at[me], gram_send.at[d], gram_recv.at[me], place(1, spot + d))
            copy.start()
            sends.append(copy)
        upper.wait_recv()
        filter_rows(mate, other, 0, split)
        for d in range(1, 2 * n_plane):
            source = (me + d) % (2 * n_plane)
            remote(
                partial.at[1], grams.at[source], gram_send.at[0], gram_recv.at[source],
                place(source // n_plane, source),
            ).wait_recv()
        spread = spread_out(grams)
        gram = {}
        for p, (i, j) in enumerate(pairs):
            gram[i, j] = spread[p:p + 1]
            q = n_self + n_cross + p
            gram[count + i, count + j] = spread[q:q + 1]
        for i in range(count):
            for j in range(count):
                p = n_self + i * count + j
                gram[count + i, j] = spread[p:p + 1]
        keep_factor(gram, 2 * count)
        finish(count, [other, filt])
        for copy in [back] + sends:
            copy.wait_send()

    for copy in stores:
        copy.wait()


def fused_body(sizes, vectors, levels, level_table, filter_low, filter_high):
    count, rows, cols = vectors.shape
    n_plane = sizes[0] * sizes[1]
    high, wide = rows + 2 * SUB, cols + 2 * LANE
    depth = -(-count * (2 * count + 1) // SUB) * SUB
    packed_rows = -(-(2 * count + 1) // SUB) * SUB
    fold_rows = -(-(high // SUB) // (LANE // (4 * count))) * SUB
    f32 = jnp.float32
    anywhere = pl.BlockSpec(memory_space=pl.ANY)
    in_smem = pl.BlockSpec(memory_space=pltpu.SMEM)
    dma = pltpu.SemaphoreType.DMA
    block = (count, rows, cols)
    padded = (count, high, wide)
    vmem_shapes = [
        padded, None, (high, wide), block, padded, block, block,
        (2, packed_rows, cols), (2, packed_rows, cols), (2, rows, LANE), (2, high, LANE),
        (fold_rows, LANE), (2, 2 * count, cols), (fold_rows, LANE), (high, LANE),
        (depth, LANE), (2, 1, LANE), (n_plane, 1, LANE), (2 * n_plane, 1, LANE),
        (2 * count, 2 * count, 1, LANE),
    ]
    scratch = [pltpu.VMEM(s, f32) if s else pltpu.VMEM((rows, cols), jnp.int32) for s in vmem_shapes]
    counts = (2 + count, 8, 8, 6, 6, n_plane, n_plane, n_plane, 2 * n_plane, 2)
    return pl.pallas_call(
        functools.partial(kernel, sizes),
        out_shape=jax.ShapeDtypeStruct(block, f32),
        in_specs=[anywhere] * 3 + [in_smem] * 2,
        out_specs=anywhere,
        scratch_shapes=[pltpu.SMEM(level_table.shape, f32)] + scratch + [dma((n,)) for n in counts],
        compiler_params=pltpu.CompilerParams(
            collective_id=0, has_side_effects=True, vmem_limit_bytes=60 * 1024 * 1024
        ),
    )(vectors, levels, level_table, filter_low, filter_high)


def solution(mesh):
    in_specs = (P("grp", "lx", "ly"), P("lx", "ly"), P(), P(), P())
    out_specs = P("grp", "lx", "ly")
    if mesh.shape["grp"] == 2:
        body = functools.partial(fused_body, (mesh.shape["lx"], mesh.shape["ly"]))
    else:
        body = general_body
    return jax.shard_map(body, mesh=mesh, in_specs=in_specs, out_specs=out_specs, check_vma=False)
```

```python
import functools

import jax
import jax.numpy as jnp
from jax import lax
from jax.experimental import pallas as pl
from jax.experimental.pallas import tpu as pltpu
from jax.sharding import PartitionSpec as P

MESH_IDS = pl.DeviceIdType.MESH
SUB, LANE = 8, 128


def padded_2(shard, sides, width):
    for axis, dim in sides:
        size, length = (lax.axis_size(axis), shard.shape[dim])
        up = [(i, (i + 1) % size) for i in range(size)]
        down = [(j, i) for i, j in up]
        last = lax.slice_in_dim(shard, length - width, length, axis=dim)
        leading = lax.slice_in_dim(shard, 0, width, axis=dim)
        before = lax.ppermute(last, axis, up)
        after = lax.ppermute(leading, axis, down)
        shard = jnp.concatenate([before, shard, after], axis=dim)
    return shard


def from_root(value, axis, source):
    kept = jnp.where(lax.axis_index(axis) == source, value, 0).astype(value.dtype)
    return lax.psum(kept, axis)


def apply_operator(field, onsite):
    padded = padded_2(field, (("lx", 1), ("ly", 2)), 1)
    beside = padded[:, 2:, 1:-1] + padded[:, :-2, 1:-1] + padded[:, 1:-1, 2:] + padded[:, 1:-1, :-2]
    return onsite[None] * field - beside


def lower_inverse(gram):
    lower = jnp.linalg.cholesky(gram)
    eye_block = jnp.eye(gram.shape[0], dtype=jnp.float32)
    return lax.linalg.triangular_solve(lower, eye_block, left_side=True, lower=True)


def general_body(vectors, levels, level_table, filter_low, filter_high):
    count_vec, rows_local, cols_local = vectors.shape
    level_ids = jnp.arange(level_table.shape[0], dtype=jnp.int32)
    onsite = jnp.sum(
        jnp.where(levels[None] == level_ids[:, None, None], level_table[:, None, None], 0.0), axis=0
    )
    center = (filter_high[0] + filter_low[0]) / 2.0
    half = (filter_high[0] - filter_low[0]) / 2.0
    first = (apply_operator(vectors, onsite) - center * vectors) / half
    filtered = 2.0 * (apply_operator(first, onsite) - center * first) / half - vectors
    total = rows_local * cols_local * lax.axis_size("lx") * lax.axis_size("ly")
    flat = filtered.reshape(count_vec, rows_local * cols_local)
    highest = lax.Precision.HIGHEST
    mine = lax.axis_index("grp")
    result = jnp.zeros_like(flat)
    for h in range(lax.axis_size("grp")):
        gram = lax.psum(jnp.dot(flat, flat.T, precision=highest), ("lx", "ly")) / total
        done = jnp.dot(lower_inverse(gram), flat, precision=highest)
        result = jnp.where(mine == h, done, result)
        shared = from_root(done, "grp", h)
        coeff = lax.psum(jnp.dot(shared, flat.T, precision=highest), ("lx", "ly")) / total
        later = mine > h
        flat = jnp.where(later, flat - jnp.dot(coeff.T, shared, precision=highest), flat)
    return result.reshape(count_vec, rows_local, cols_local)


def pair_rows(count):
    return [(i, j) for i in range(count) for j in range(i + 1)]


def lane_ids(shape):
    return lax.broadcasted_iota(jnp.int32, shape, len(shape) - 1)


def turned(tile, shift):
    shift = shift % LANE
    return pltpu.roll(tile, shift, 1) if shift else tile


def inverse_of_factor(gram, size):
    lower, inverse, recip = {}, {}, []
    for j in range(size):
        for i in range(j, size):
            value = gram[i, j]
            for k in range(j):
                value = value - lower[i, k] * lower[j, k]
            if i == j:
                recip.append(1.0 / jnp.sqrt(value))
            else:
                lower[i, j] = value * recip[j]
    for j in range(size):
        inverse[j, j] = recip[j]
        for i in range(j + 1, size):
            value = lower[i, j] * inverse[j, j]
            for k in range(j + 1, i):
                value = value + lower[i, k] * inverse[k, j]
            inverse[i, j] = -(value * recip[i])
    return inverse


def kernel(
    sizes, vec_hbm, lev_hbm, table_hbm, low_ref, high_ref, result,
    table_ref, field, level, onsite, filt, mate, other,
    row_send, row_recv, col_send, col_recv, edge_cols, mate_rows, mate_fold, mate_cols,
    parts, partial, early, grams, factors,
    load_sem, halo_send, halo_recv, grp_send, grp_recv, early_send, early_recv, gram_send, gram_recv,
):
    n_lx, n_ly = sizes
    count, rows, cols = vec_hbm.shape
    n_levels = table_hbm.shape[0]
    grp, lx, ly = lax.axis_index("grp"), lax.axis_index("lx"), lax.axis_index("ly")
    n_plane = n_lx * n_ly
    spot = lx * n_ly + ly
    me = grp * n_plane + spot
    r0, r1, c0, c1 = SUB, SUB + rows, LANE, LANE + cols
    high, wide = r1 + SUB, c1 + LANE
    split = rows // 2 // SUB * SUB
    group = 2 * SUB
    per_tile = LANE // group
    bands = rows // SUB

    def place(block, index):
        index = index % n_plane
        return (block, index // n_ly, index % n_ly)

    def remote(src, dst, send, recv, to):
        return pltpu.make_async_remote_copy(
            src_ref=src, dst_ref=dst, send_sem=send, recv_sem=recv, device_id=to, device_id_type=MESH_IDS
        )

    loads = [pltpu.make_async_copy(lev_hbm, level, load_sem.at[0])]
    loads += [pltpu.make_async_copy(table_hbm, table_ref, load_sem.at[1])]
    loads += [
        pltpu.make_async_copy(vec_hbm.at[v], field.at[v, pl.ds(r0, rows), pl.ds(c0, cols)], load_sem.at[2 + v])
        for v in range(count)
    ]
    for copy in loads:
        copy.start()

    barrier = pltpu.get_barrier_semaphore()
    for d in range(1, n_plane):
        pl.semaphore_signal(barrier, inc=1, device_id=place(grp, spot + d), device_id_type=MESH_IDS)
    pl.semaphore_signal(barrier, inc=1, device_id=(1 - grp, lx, ly), device_id_type=MESH_IDS)

    @pl.when(grp == 1)
    def _():
        for d in range(1, n_plane):
            pl.semaphore_signal(barrier, inc=1, device_id=place(0, spot + d), device_id_type=MESH_IDS)

    for copy in loads:
        copy.wait()

    lev = level[...]
    site = jnp.zeros(lev.shape, jnp.float32)
    for k in range(n_levels):
        site = jnp.where(lev == k, table_ref[k], site)
    onsite[r0:r1, c0:c1] = site
    for v in range(count):
        row_send[0, 2 * v:2 * v + 2, :] = field[v, r1 - 2:r1, c0:c1]
        row_send[1, 2 * v:2 * v + 2, :] = field[v, r0:r0 + 2, c0:c1]
    row_send[0, 2 * count:2 * count + 1, :] = onsite[r1 - 1:r1, c0:c1]
    row_send[1, 2 * count:2 * count + 1, :] = onsite[r0:r0 + 1, c0:c1]
    lanes = lane_ids((rows, LANE))
    ends = onsite[r0:r1, c1 - LANE:c1]
    begins = onsite[r0:r1, c0:c0 + LANE]
    right = pltpu.roll(ends, LANE - 2 * count, 1)
    left = pltpu.roll(begins, 2 * count, 1)
    for v in range(count):
        here = field[v, r0:r1, c1 - LANE:c1]
        here = here if v == 0 else pltpu.roll(here, LANE - 2 * v, 1)
        right = jnp.where((lanes >= LANE - 2 - 2 * v) & (lanes < LANE - 2 * v), here, right)
        here = field[v, r0:r1, c0:c0 + LANE]
        here = here if v == 0 else pltpu.roll(here, 2 * v, 1)
        left = jnp.where((lanes >= 2 * v) & (lanes < 2 * v + 2), here, left)
    tile_lanes = lane_ids((SUB, LANE))
    for side, edge in enumerate((right, left)):
        for t in range(col_send.shape[1] // SUB):
            value = jnp.zeros((SUB, LANE), jnp.float32)
            for k in range(t * per_tile, min(bands, (t + 1) * per_tile)):
                at = group * (k - t * per_tile)
                tile = turned(edge[k * SUB:(k + 1) * SUB], at + group * (1 - side))
                value = jnp.where((tile_lanes >= at) & (tile_lanes < at + group), tile, value)
            col_send[side, t * SUB:(t + 1) * SUB] = value

    @pl.when(grp == 0)
    def _():
        pl.semaphore_wait(barrier, 2 * n_plane - 1)

    @pl.when(grp == 1)
    def _():
        pl.semaphore_wait(barrier, n_plane)

    up, down = (lx + n_lx - 1) % n_lx, (lx + 1) % n_lx
    west, east = (ly + n_ly - 1) % n_ly, (ly + 1) % n_ly
    halos = []

    def halo(src, dst, x, y):
        k = len(halos)
        copy = remote(src, dst, halo_send.at[k], halo_recv.at[k], (grp, x, y))
        copy.start()
        halos.append(copy)

    for side, y in ((0, east), (1, west)):
        for slot, x in enumerate((lx, down, up)):
            halo(col_send.at[side], col_recv.at[side, slot], x, y)
    halo(row_send.at[0], row_recv.at[0], down, ly)
    halo(row_send.at[1], row_recv.at[1], up, ly)

    partner = (1 - grp, lx, ly)
    n_link = [0]

    def across(src, dst):
        k = n_link[0]
        n_link[0] += 1
        return remote(src, dst, grp_send.at[k], grp_recv.at[k], partner)

    def band(start, stop):
        at = (slice(None), pl.ds(r0 + start, stop - start), pl.ds(c0, cols))
        return across(field.at[at], mate.at[at])

    lower = band(split - SUB, rows)
    upper = band(0, split - SUB)
    back = band(0, split + SUB)
    edges = [across(row_recv.at[:, pl.ds(0, 2 * count)], mate_rows), across(col_recv, mate_fold)]

    @pl.when(grp == 0)
    def _():
        lower.start()

    @pl.when(grp == 1)
    def _():
        back.start()

    for copy in halos:
        copy.wait()

    for copy in edges:
        copy.start()

    @pl.when(grp == 0)
    def _():
        upper.start()

    def unfold(src, dst):
        for side in range(2):
            for k in range(bands + 2):
                slot, band_at = (1, bands - 1) if k == 0 else (2, 0) if k == bands + 1 else (0, k - 1)
                t, g = band_at // per_tile, band_at % per_tile
                tile = src[side, slot, t * SUB:(t + 1) * SUB]
                dst[side, k * SUB:(k + 1) * SUB] = turned(tile, -group * (g + 1 - side))

    def place_edges(dst, first_rows, last_rows, before, after):
        for v in range(count):
            dst[v, r0 - 2:r0, c0:c1] = first_rows[2 * v:2 * v + 2, :]
            dst[v, r1:r1 + 2, c0:c1] = last_rows[2 * v:2 * v + 2, :]
            dst[v, :, 0:LANE] = pltpu.roll(before[...], 2 * v, 1) if v else before[...]
            dst[v, :, c1:c1 + LANE] = pltpu.roll(after[...], LANE - 2 * v, 1) if v else after[...]

    unfold(col_recv, edge_cols)
    place_edges(field, row_recv.at[0], row_recv.at[1], edge_cols.at[0], edge_cols.at[1])
    low = jnp.full((1, 1), low_ref[0], jnp.float32)
    top = jnp.full((1, 1), high_ref[0], jnp.float32)
    center = (top + low) * 0.5
    scale = 2.0 / (top - low)
    onsite[r0 - 1:r0, c0:c1] = row_recv[0, 2 * count:2 * count + 1, :]
    onsite[r1:r1 + 1, c0:c1] = row_recv[1, 2 * count:2 * count + 1, :]
    onsite[:, 0:LANE] = pltpu.roll(edge_cols[0], 2 * count, 1)
    onsite[:, c1:c1 + LANE] = pltpu.roll(edge_cols[1], LANE - 2 * count, 1)
    onsite[...] = (onsite[...] - center) * scale

    def filter_rows(src, dst, start, stop):
        at = pl.ds(start, stop - start + 2 * SUB)
        n = stop - start + 2 * SUB
        diagonal = onsite[at, :]

        def beside(x):
            return (pltpu.roll(x, 1, 0) + pltpu.roll(x, n - 1, 0)
                    + pltpu.roll(x, 1, 1) + pltpu.roll(x, wide - 1, 1))

        for v in range(count):
            x = src[v, at, :]
            first = diagonal * x - beside(x) * scale
            second = 2.0 * (diagonal * first - beside(first) * scale) - x
            dst[v, start:stop] = second[SUB:SUB + stop - start, c0:c1]

    filter_rows(field, filt, 0, rows)

    pairs = pair_rows(count)
    n_self, n_cross = len(pairs), count * count
    depth = parts.shape[0]
    diag = lane_ids((depth, LANE)) == lax.broadcasted_iota(jnp.int32, (depth, LANE), 0)
    total = rows * cols * n_lx * n_ly

    def folded(a, b):
        prod = a * b
        acc = prod[:, 0:LANE]
        for k in range(1, cols // LANE):
            acc = acc + prod[:, k * LANE:(k + 1) * LANE]
        return jnp.sum(acc, axis=0, keepdims=True)

    def packed_parts():
        sums = jnp.sum(parts[...], axis=1, keepdims=True)
        return jnp.sum(jnp.where(diag, sums, 0.0), axis=0, keepdims=True)

    def spread_out(slots):
        whole = jnp.sum(slots[...], axis=0) / total
        column = jnp.sum(jnp.where(diag, whole, 0.0), axis=1, keepdims=True)
        return jnp.broadcast_to(column, (depth, LANE))

    def keep_factor(gram, size):
        for (i, j), value in inverse_of_factor(gram, size).items():
            factors[i, j] = value

    parts[...] = jnp.zeros(parts.shape, jnp.float32)
    for p, (i, j) in enumerate(pairs):
        value = folded(filt[i], filt[j])
        parts[p:p + 1, :] = jnp.where(grp == 0, value, 0.0)
        q = n_self + n_cross + p
        parts[q:q + 1, :] = jnp.where(grp == 0, 0.0, value)

    def cross_parts(block_0, block_1, start, stop):
        for i in range(count):
            for j in range(count):
                p = n_self + i * count + j
                parts[p:p + 1, :] = folded(block_1[i, start:stop], block_0[j, start:stop])

    def combine(start, stop, first_row, blocks):
        for at_row in range(start, stop, SUB):
            at = pl.ds(at_row, SUB)
            for t in range(cols // LANE):
                on = pl.ds(t * LANE, LANE)
                tiles = [block[v, at, on] for block in blocks for v in range(count)]
                for i in range(count):
                    row = first_row + i
                    value = factors[row, 0] * tiles[0]
                    for j in range(1, row + 1):
                        value = value + factors[row, j] * tiles[j]
                    result[i, at, on] = value

    def place_mate_edges():
        for copy in edges:
            copy.wait_recv()
        unfold(mate_fold, mate_cols)
        place_edges(mate, mate_rows.at[0], mate_rows.at[1], mate_cols.at[0], mate_cols.at[1])

    @pl.when(grp == 0)
    def _():
        partial[0] = packed_parts()
        early[spot] = partial[0]
        sends = []
        for d in range(1, n_plane):
            copy = remote(partial.at[0], early.at[spot], early_send.at[d], early_recv.at[spot], place(0, spot + d))
            copy.start()
            sends.append(copy)
        place_mate_edges()
        back.wait_recv()
        filter_rows(mate, other, 0, split)
        cross_parts(filt, other, 0, split)
        partial[1] = packed_parts()
        for d in range(n_plane):
            copy = remote(partial.at[1], grams.at[me], gram_send.at[d], gram_recv.at[me], place(1, spot + d))
            copy.start()
            sends.append(copy)
        for d in range(1, n_plane):
            source = (spot + d) % n_plane
            remote(partial.at[0], early.at[source], early_send.at[d], early_recv.at[source], place(0, source)).wait_recv()
        spread = spread_out(early)
        keep_factor({(i, j): spread[p:p + 1] for p, (i, j) in enumerate(pairs)}, count)
        combine(0, rows, 0, [filt])
        for copy in [lower, upper] + edges + sends:
            copy.wait_send()

    @pl.when(grp == 1)
    def _():
        place_mate_edges()
        lower.wait_recv()
        filter_rows(mate, other, split, rows)
        cross_parts(other, filt, split, rows)
        partial[1] = packed_parts()
        grams[me] = partial[1]
        sends = []
        for d in range(1, n_plane):
            copy = remote(partial.at[1], grams.at[me], gram_send.at[d], gram_recv.at[me], place(1, spot + d))
            copy.start()
            sends.append(copy)
        upper.wait_recv()
        filter_rows(mate, other, 0, split)
        for d in range(1, 2 * n_plane):
            source = (me + d) % (2 * n_plane)
            remote(
                partial.at[1], grams.at[source], gram_send.at[0], gram_recv.at[source],
                place(source // n_plane, source),
            ).wait_recv()
        spread = spread_out(grams)
        gram = {}
        for p, (i, j) in enumerate(pairs):
            gram[i, j] = spread[p:p + 1]
            q = n_self + n_cross + p
            gram[count + i, count + j] = spread[q:q + 1]
        for i in range(count):
            for j in range(count):
                p = n_self + i * count + j
                gram[count + i, j] = spread[p:p + 1]
        keep_factor(gram, 2 * count)
        combine(0, rows, count, [other, filt])
        for copy in [back] + edges + sends:
            copy.wait_send()


def fused_body(sizes, vectors, levels, level_table, filter_low, filter_high):
    count, rows, cols = vectors.shape
    n_plane = sizes[0] * sizes[1]
    high, wide = rows + 2 * SUB, cols + 2 * LANE
    depth = -(-count * (2 * count + 1) // SUB) * SUB
    packed_rows = -(-(2 * count + 1) // SUB) * SUB
    fold_rows = -(-(rows // SUB) // (LANE // (2 * SUB))) * SUB
    f32 = jnp.float32
    anywhere = pl.BlockSpec(memory_space=pl.ANY)
    in_smem = pl.BlockSpec(memory_space=pltpu.SMEM)
    dma = pltpu.SemaphoreType.DMA
    block = (count, rows, cols)
    padded = (count, high, wide)
    vmem_shapes = [
        padded, None, (high, wide), block, padded, block,
        (2, packed_rows, cols), (2, packed_rows, cols), (2, fold_rows, LANE), (2, 3, fold_rows, LANE),
        (2, high, LANE), (2, 2 * count, cols), (2, 3, fold_rows, LANE), (2, high, LANE),
        (depth, LANE), (2, 1, LANE), (n_plane, 1, LANE), (2 * n_plane, 1, LANE),
        (2 * count, 2 * count, 1, LANE),
    ]
    scratch = [pltpu.VMEM(s, f32) if s else pltpu.VMEM((rows, cols), jnp.int32) for s in vmem_shapes]
    counts = (2 + count, 8, 8, 5, 5, n_plane, n_plane, n_plane, 2 * n_plane)
    return pl.pallas_call(
        functools.partial(kernel, sizes),
        out_shape=pltpu.VMEM(block, f32),
        in_specs=[anywhere] * 3 + [in_smem] * 2,
        out_specs=pl.BlockSpec(memory_space=pltpu.VMEM),
        scratch_shapes=[pltpu.SMEM(level_table.shape, f32)] + scratch + [dma((n,)) for n in counts],
        compiler_params=pltpu.CompilerParams(
            collective_id=0, has_side_effects=True, vmem_limit_bytes=60 * 1024 * 1024
        ),
    )(vectors, levels, level_table, filter_low, filter_high)


def solution(mesh):
    in_specs = (P("grp", "lx", "ly"), P("lx", "ly"), P(), P(), P())
    out_specs = P("grp", "lx", "ly")
    if mesh.shape["grp"] == 2:
        body = functools.partial(fused_body, (mesh.shape["lx"], mesh.shape["ly"]))
    else:
        body = general_body
    return jax.shard_map(body, mesh=mesh, in_specs=in_specs, out_specs=out_specs, check_vma=False)
```

```python
import functools

import jax
import jax.numpy as jnp
from jax import lax
from jax.experimental import pallas as pl
from jax.experimental.pallas import tpu as pltpu
from jax.sharding import PartitionSpec as P

MESH_IDS = pl.DeviceIdType.MESH
SUB, LANE = 8, 128


def padded_2(shard, sides, width):
    for axis, dim in sides:
        size, length = (lax.axis_size(axis), shard.shape[dim])
        up = [(i, (i + 1) % size) for i in range(size)]
        down = [(j, i) for i, j in up]
        last = lax.slice_in_dim(shard, length - width, length, axis=dim)
        leading = lax.slice_in_dim(shard, 0, width, axis=dim)
        before = lax.ppermute(last, axis, up)
        after = lax.ppermute(leading, axis, down)
        shard = jnp.concatenate([before, shard, after], axis=dim)
    return shard


def from_root(value, axis, source):
    kept = jnp.where(lax.axis_index(axis) == source, value, 0).astype(value.dtype)
    return lax.psum(kept, axis)


def apply_operator(field, onsite):
    padded = padded_2(field, (("lx", 1), ("ly", 2)), 1)
    beside = padded[:, 2:, 1:-1] + padded[:, :-2, 1:-1] + padded[:, 1:-1, 2:] + padded[:, 1:-1, :-2]
    return onsite[None] * field - beside


def lower_inverse(gram):
    lower = jnp.linalg.cholesky(gram)
    eye_block = jnp.eye(gram.shape[0], dtype=jnp.float32)
    return lax.linalg.triangular_solve(lower, eye_block, left_side=True, lower=True)


def general_body(vectors, levels, level_table, filter_low, filter_high):
    count_vec, rows_local, cols_local = vectors.shape
    level_ids = jnp.arange(level_table.shape[0], dtype=jnp.int32)
    onsite = jnp.sum(
        jnp.where(levels[None] == level_ids[:, None, None], level_table[:, None, None], 0.0), axis=0
    )
    center = (filter_high[0] + filter_low[0]) / 2.0
    half = (filter_high[0] - filter_low[0]) / 2.0
    first = (apply_operator(vectors, onsite) - center * vectors) / half
    filtered = 2.0 * (apply_operator(first, onsite) - center * first) / half - vectors
    total = rows_local * cols_local * lax.axis_size("lx") * lax.axis_size("ly")
    flat = filtered.reshape(count_vec, rows_local * cols_local)
    highest = lax.Precision.HIGHEST
    mine = lax.axis_index("grp")
    result = jnp.zeros_like(flat)
    for h in range(lax.axis_size("grp")):
        gram = lax.psum(jnp.dot(flat, flat.T, precision=highest), ("lx", "ly")) / total
        done = jnp.dot(lower_inverse(gram), flat, precision=highest)
        result = jnp.where(mine == h, done, result)
        shared = from_root(done, "grp", h)
        coeff = lax.psum(jnp.dot(shared, flat.T, precision=highest), ("lx", "ly")) / total
        later = mine > h
        flat = jnp.where(later, flat - jnp.dot(coeff.T, shared, precision=highest), flat)
    return result.reshape(count_vec, rows_local, cols_local)


def pair_rows(count):
    return [(i, j) for i in range(count) for j in range(i + 1)]


def lane_ids(shape):
    return lax.broadcasted_iota(jnp.int32, shape, len(shape) - 1)


def turned(tile, shift):
    shift = shift % LANE
    return pltpu.roll(tile, shift, 1) if shift else tile


def inverse_of_factor(gram, size):
    lower, inverse, recip = {}, {}, []
    for j in range(size):
        for i in range(j, size):
            value = gram[i, j]
            for k in range(j):
                value = value - lower[i, k] * lower[j, k]
            if i == j:
                recip.append(1.0 / jnp.sqrt(value))
            else:
                lower[i, j] = value * recip[j]
    for j in range(size):
        inverse[j, j] = recip[j]
        for i in range(j + 1, size):
            value = lower[i, j] * inverse[j, j]
            for k in range(j + 1, i):
                value = value + lower[i, k] * inverse[k, j]
            inverse[i, j] = -(value * recip[i])
    return inverse


def kernel(
    sizes, vec_hbm, lev_hbm, table_hbm, low_ref, high_ref, result,
    table_ref, field, level, onsite, filt, mate, other,
    row_send, row_recv, col_send, col_recv, edge_cols, mate_rows, mate_fold, mate_cols,
    parts, partial, early, grams, factors,
    load_sem, halo_send, halo_recv, grp_send, grp_recv, early_send, early_recv, gram_send, gram_recv,
):
    n_lx, n_ly = sizes
    count, rows, cols = vec_hbm.shape
    n_levels = table_hbm.shape[0]
    grp, lx, ly = lax.axis_index("grp"), lax.axis_index("lx"), lax.axis_index("ly")
    n_plane = n_lx * n_ly
    spot = lx * n_ly + ly
    me = grp * n_plane + spot
    r0, r1, c0, c1 = SUB, SUB + rows, LANE, LANE + cols
    high, wide = r1 + SUB, c1 + LANE
    split = rows // 2 // SUB * SUB
    last = split // 2 // SUB * SUB
    group = 2 * SUB
    per_tile = LANE // group
    bands = rows // SUB

    def place(block, index):
        index = index % n_plane
        return (block, index // n_ly, index % n_ly)

    def remote(src, dst, send, recv, to):
        return pltpu.make_async_remote_copy(
            src_ref=src, dst_ref=dst, send_sem=send, recv_sem=recv, device_id=to, device_id_type=MESH_IDS
        )

    loads = [pltpu.make_async_copy(lev_hbm, level, load_sem.at[0])]
    loads += [pltpu.make_async_copy(table_hbm, table_ref, load_sem.at[1])]
    loads += [
        pltpu.make_async_copy(vec_hbm.at[v], field.at[v, pl.ds(r0, rows), pl.ds(c0, cols)], load_sem.at[2 + v])
        for v in range(count)
    ]
    for copy in loads[2:] + loads[:2]:
        copy.start()

    barrier = pltpu.get_barrier_semaphore()
    for d in range(1, n_plane):
        pl.semaphore_signal(barrier, inc=1, device_id=place(grp, spot + d), device_id_type=MESH_IDS)
    pl.semaphore_signal(barrier, inc=1, device_id=(1 - grp, lx, ly), device_id_type=MESH_IDS)

    @pl.when(grp == 1)
    def _():
        for d in range(1, n_plane):
            pl.semaphore_signal(barrier, inc=1, device_id=place(0, spot + d), device_id_type=MESH_IDS)

    for copy in loads[2:]:
        copy.wait()

    @pl.when(grp == 0)
    def _():
        pl.semaphore_wait(barrier, 2 * n_plane - 1)

    @pl.when(grp == 1)
    def _():
        pl.semaphore_wait(barrier, n_plane)

    partner = (1 - grp, lx, ly)
    n_link = [0]

    def across(src, dst):
        k = n_link[0]
        n_link[0] += 1
        return remote(src, dst, grp_send.at[k], grp_recv.at[k], partner)

    def band(start, stop):
        at = (slice(None), pl.ds(r0 + start, stop - start), pl.ds(c0, cols))
        return across(field.at[at], mate.at[at])

    lower = band(split - SUB, rows)
    middle = band(last - SUB, split - SUB)
    upper = band(0, last - SUB)
    back = band(0, split + SUB)
    edges = [across(row_recv.at[:, pl.ds(0, 2 * count)], mate_rows), across(col_recv, mate_fold)]

    @pl.when(grp == 0)
    def _():
        lower.start()

    @pl.when(grp == 1)
    def _():
        back.start()

    for copy in loads[:2]:
        copy.wait()

    lev = level[...]
    site = jnp.zeros(lev.shape, jnp.float32)
    for k in range(n_levels):
        site = jnp.where(lev == k, table_ref[k], site)
    onsite[r0:r1, c0:c1] = site
    for v in range(count):
        row_send[0, 2 * v:2 * v + 2, :] = field[v, r1 - 2:r1, c0:c1]
        row_send[1, 2 * v:2 * v + 2, :] = field[v, r0:r0 + 2, c0:c1]
    row_send[0, 2 * count:2 * count + 1, :] = onsite[r1 - 1:r1, c0:c1]
    row_send[1, 2 * count:2 * count + 1, :] = onsite[r0:r0 + 1, c0:c1]
    lanes = lane_ids((rows, LANE))
    ends = onsite[r0:r1, c1 - LANE:c1]
    begins = onsite[r0:r1, c0:c0 + LANE]
    right = pltpu.roll(ends, LANE - 2 * count, 1)
    left = pltpu.roll(begins, 2 * count, 1)
    for v in range(count):
        here = field[v, r0:r1, c1 - LANE:c1]
        here = here if v == 0 else pltpu.roll(here, LANE - 2 * v, 1)
        right = jnp.where((lanes >= LANE - 2 - 2 * v) & (lanes < LANE - 2 * v), here, right)
        here = field[v, r0:r1, c0:c0 + LANE]
        here = here if v == 0 else pltpu.roll(here, 2 * v, 1)
        left = jnp.where((lanes >= 2 * v) & (lanes < 2 * v + 2), here, left)
    tile_lanes = lane_ids((SUB, LANE))
    for side, edge in enumerate((right, left)):
        for t in range(col_send.shape[1] // SUB):
            value = jnp.zeros((SUB, LANE), jnp.float32)
            for k in range(t * per_tile, min(bands, (t + 1) * per_tile)):
                at = group * (k - t * per_tile)
                tile = turned(edge[k * SUB:(k + 1) * SUB], at + group * (1 - side))
                value = jnp.where((tile_lanes >= at) & (tile_lanes < at + group), tile, value)
            col_send[side, t * SUB:(t + 1) * SUB] = value

    up, down = (lx + n_lx - 1) % n_lx, (lx + 1) % n_lx
    west, east = (ly + n_ly - 1) % n_ly, (ly + 1) % n_ly
    halos = []

    def halo(src, dst, x, y):
        k = len(halos)
        copy = remote(src, dst, halo_send.at[k], halo_recv.at[k], (grp, x, y))
        copy.start()
        halos.append(copy)

    for side, y in ((0, east), (1, west)):
        for slot, x in enumerate((lx, down, up)):
            halo(col_send.at[side], col_recv.at[side, slot], x, y)
    halo(row_send.at[0], row_recv.at[0], down, ly)
    halo(row_send.at[1], row_recv.at[1], up, ly)

    for copy in halos:
        copy.wait()

    for copy in edges:
        copy.start()

    @pl.when(grp == 0)
    def _():
        middle.start()
        upper.start()

    def unfold(src, dst):
        for side in range(2):
            for k in range(bands + 2):
                slot, band_at = (1, bands - 1) if k == 0 else (2, 0) if k == bands + 1 else (0, k - 1)
                t, g = band_at // per_tile, band_at % per_tile
                tile = src[side, slot, t * SUB:(t + 1) * SUB]
                dst[side, k * SUB:(k + 1) * SUB] = turned(tile, -group * (g + 1 - side))

    def place_edges(dst, first_rows, last_rows, before, after):
        for v in range(count):
            dst[v, r0 - 2:r0, c0:c1] = first_rows[2 * v:2 * v + 2, :]
            dst[v, r1:r1 + 2, c0:c1] = last_rows[2 * v:2 * v + 2, :]
            dst[v, :, 0:LANE] = pltpu.roll(before[...], 2 * v, 1) if v else before[...]
            dst[v, :, c1:c1 + LANE] = pltpu.roll(after[...], LANE - 2 * v, 1) if v else after[...]

    unfold(col_recv, edge_cols)
    place_edges(field, row_recv.at[0], row_recv.at[1], edge_cols.at[0], edge_cols.at[1])
    low = jnp.full((1, 1), low_ref[0], jnp.float32)
    top = jnp.full((1, 1), high_ref[0], jnp.float32)
    center = (top + low) * 0.5
    scale = 2.0 / (top - low)
    onsite[r0 - 1:r0, c0:c1] = row_recv[0, 2 * count:2 * count + 1, :]
    onsite[r1:r1 + 1, c0:c1] = row_recv[1, 2 * count:2 * count + 1, :]
    onsite[:, 0:LANE] = pltpu.roll(edge_cols[0], 2 * count, 1)
    onsite[:, c1:c1 + LANE] = pltpu.roll(edge_cols[1], LANE - 2 * count, 1)
    onsite[...] = (onsite[...] - center) * scale

    def filter_rows(src, dst, start, stop):
        at = pl.ds(start, stop - start + 2 * SUB)
        n = stop - start + 2 * SUB
        diagonal = onsite[at, :]

        def beside(x):
            return (pltpu.roll(x, 1, 0) + pltpu.roll(x, n - 1, 0)
                    + pltpu.roll(x, 1, 1) + pltpu.roll(x, wide - 1, 1))

        for v in range(count):
            x = src[v, at, :]
            first = diagonal * x - beside(x) * scale
            second = 2.0 * (diagonal * first - beside(first) * scale) - x
            dst[v, start:stop] = second[SUB:SUB + stop - start, c0:c1]

    filter_rows(field, filt, 0, rows)

    pairs = pair_rows(count)
    n_self, n_cross = len(pairs), count * count
    depth = parts.shape[0]
    diag = lane_ids((depth, LANE)) == lax.broadcasted_iota(jnp.int32, (depth, LANE), 0)
    total = rows * cols * n_lx * n_ly

    def folded(a, b):
        prod = a * b
        acc = prod[:, 0:LANE]
        for k in range(1, cols // LANE):
            acc = acc + prod[:, k * LANE:(k + 1) * LANE]
        return jnp.sum(acc, axis=0, keepdims=True)

    def packed_parts():
        sums = jnp.sum(parts[...], axis=1, keepdims=True)
        return jnp.sum(jnp.where(diag, sums, 0.0), axis=0, keepdims=True)

    def spread_out(slots):
        whole = jnp.sum(slots[...], axis=0) / total
        column = jnp.sum(jnp.where(diag, whole, 0.0), axis=1, keepdims=True)
        return jnp.broadcast_to(column, (depth, LANE))

    def keep_factor(gram, size):
        for (i, j), value in inverse_of_factor(gram, size).items():
            factors[i, j] = value

    parts[...] = jnp.zeros(parts.shape, jnp.float32)
    for p, (i, j) in enumerate(pairs):
        value = folded(filt[i], filt[j])
        parts[p:p + 1, :] = jnp.where(grp == 0, value, 0.0)
        q = n_self + n_cross + p
        parts[q:q + 1, :] = jnp.where(grp == 0, 0.0, value)

    def cross_parts(block_0, block_1, start, stop):
        for i in range(count):
            for j in range(count):
                p = n_self + i * count + j
                parts[p:p + 1, :] = folded(block_1[i, start:stop], block_0[j, start:stop])

    def combine(start, stop, first_row, blocks):
        for at_row in range(start, stop, SUB):
            at = pl.ds(at_row, SUB)
            for t in range(cols // LANE):
                on = pl.ds(t * LANE, LANE)
                tiles = [block[v, at, on] for block in blocks for v in range(count)]
                for i in range(count):
                    row = first_row + i
                    value = factors[row, 0] * tiles[0]
                    for j in range(1, row + 1):
                        value = value + factors[row, j] * tiles[j]
                    result[i, at, on] = value

    def place_mate_edges():
        for copy in edges:
            copy.wait_recv()
        unfold(mate_fold, mate_cols)
        place_edges(mate, mate_rows.at[0], mate_rows.at[1], mate_cols.at[0], mate_cols.at[1])

    @pl.when(grp == 0)
    def _():
        partial[0] = packed_parts()
        early[spot] = partial[0]
        sends = []
        for d in range(1, n_plane):
            copy = remote(partial.at[0], early.at[spot], early_send.at[d], early_recv.at[spot], place(0, spot + d))
            copy.start()
            sends.append(copy)
        place_mate_edges()
        back.wait_recv()
        filter_rows(mate, other, 0, split)
        cross_parts(filt, other, 0, split)
        partial[1] = packed_parts()
        for d in range(n_plane):
            copy = remote(partial.at[1], grams.at[me], gram_send.at[d], gram_recv.at[me], place(1, spot + d))
            copy.start()
            sends.append(copy)
        for d in range(1, n_plane):
            source = (spot + d) % n_plane
            remote(partial.at[0], early.at[source], early_send.at[d], early_recv.at[source], place(0, source)).wait_recv()
        spread = spread_out(early)
        keep_factor({(i, j): spread[p:p + 1] for p, (i, j) in enumerate(pairs)}, count)
        combine(0, rows, 0, [filt])
        for copy in [lower, middle, upper] + edges + sends:
            copy.wait_send()

    @pl.when(grp == 1)
    def _():
        place_mate_edges()
        lower.wait_recv()
        filter_rows(mate, other, split, rows)
        cross_parts(other, filt, split, rows)
        partial[1] = packed_parts()
        grams[me] = partial[1]
        sends = []
        for d in range(1, n_plane):
            copy = remote(partial.at[1], grams.at[me], gram_send.at[d], gram_recv.at[me], place(1, spot + d))
            copy.start()
            sends.append(copy)
        middle.wait_recv()
        filter_rows(mate, other, last, split)
        for d in range(1, 2 * n_plane):
            source = (me + d) % (2 * n_plane)
            remote(
                partial.at[1], grams.at[source], gram_send.at[0], gram_recv.at[source],
                place(source // n_plane, source),
            ).wait_recv()
        spread = spread_out(grams)
        gram = {}
        for p, (i, j) in enumerate(pairs):
            gram[i, j] = spread[p:p + 1]
            q = n_self + n_cross + p
            gram[count + i, count + j] = spread[q:q + 1]
        for i in range(count):
            for j in range(count):
                p = n_self + i * count + j
                gram[count + i, j] = spread[p:p + 1]
        keep_factor(gram, 2 * count)
        combine(last, rows, count, [other, filt])
        upper.wait_recv()
        filter_rows(mate, other, 0, last)
        combine(0, last, count, [other, filt])
        for copy in [back] + edges + sends:
            copy.wait_send()


def fused_body(sizes, vectors, levels, level_table, filter_low, filter_high):
    count, rows, cols = vectors.shape
    n_plane = sizes[0] * sizes[1]
    high, wide = rows + 2 * SUB, cols + 2 * LANE
    depth = -(-count * (2 * count + 1) // SUB) * SUB
    packed_rows = -(-(2 * count + 1) // SUB) * SUB
    fold_rows = -(-(rows // SUB) // (LANE // (2 * SUB))) * SUB
    f32 = jnp.float32
    anywhere = pl.BlockSpec(memory_space=pl.ANY)
    in_smem = pl.BlockSpec(memory_space=pltpu.SMEM)
    dma = pltpu.SemaphoreType.DMA
    block = (count, rows, cols)
    padded = (count, high, wide)
    vmem_shapes = [
        padded, None, (high, wide), block, padded, block,
        (2, packed_rows, cols), (2, packed_rows, cols), (2, fold_rows, LANE), (2, 3, fold_rows, LANE),
        (2, high, LANE), (2, 2 * count, cols), (2, 3, fold_rows, LANE), (2, high, LANE),
        (depth, LANE), (2, 1, LANE), (n_plane, 1, LANE), (2 * n_plane, 1, LANE),
        (2 * count, 2 * count, 1, LANE),
    ]
    scratch = [pltpu.VMEM(s, f32) if s else pltpu.VMEM((rows, cols), jnp.int32) for s in vmem_shapes]
    counts = (2 + count, 8, 8, 6, 6, n_plane, n_plane, n_plane, 2 * n_plane)
    return pl.pallas_call(
        functools.partial(kernel, sizes),
        out_shape=pltpu.VMEM(block, f32),
        in_specs=[anywhere] * 3 + [in_smem] * 2,
        out_specs=pl.BlockSpec(memory_space=pltpu.VMEM),
        scratch_shapes=[pltpu.SMEM(level_table.shape, f32)] + scratch + [dma((n,)) for n in counts],
        compiler_params=pltpu.CompilerParams(
            collective_id=0, has_side_effects=True, vmem_limit_bytes=60 * 1024 * 1024
        ),
    )(vectors, levels, level_table, filter_low, filter_high)


def solution(mesh):
    in_specs = (P("grp", "lx", "ly"), P("lx", "ly"), P(), P(), P())
    out_specs = P("grp", "lx", "ly")
    if mesh.shape["grp"] == 2:
        body = functools.partial(fused_body, (mesh.shape["lx"], mesh.shape["ly"]))
    else:
        body = general_body
    return jax.shard_map(body, mesh=mesh, in_specs=in_specs, out_specs=out_specs, check_vma=False)
```

```python
import functools

import jax
import jax.numpy as jnp
from jax import lax
from jax.experimental import pallas as pl
from jax.experimental.pallas import tpu as pltpu
from jax.sharding import PartitionSpec as P

MESH_IDS = pl.DeviceIdType.MESH
SUB, LANE = 8, 128


def padded_2(shard, sides, width):
    for axis, dim in sides:
        size, length = (lax.axis_size(axis), shard.shape[dim])
        up = [(i, (i + 1) % size) for i in range(size)]
        down = [(j, i) for i, j in up]
        last = lax.slice_in_dim(shard, length - width, length, axis=dim)
        leading = lax.slice_in_dim(shard, 0, width, axis=dim)
        before = lax.ppermute(last, axis, up)
        after = lax.ppermute(leading, axis, down)
        shard = jnp.concatenate([before, shard, after], axis=dim)
    return shard


def from_root(value, axis, source):
    kept = jnp.where(lax.axis_index(axis) == source, value, 0).astype(value.dtype)
    return lax.psum(kept, axis)


def apply_operator(field, onsite):
    padded = padded_2(field, (("lx", 1), ("ly", 2)), 1)
    beside = padded[:, 2:, 1:-1] + padded[:, :-2, 1:-1] + padded[:, 1:-1, 2:] + padded[:, 1:-1, :-2]
    return onsite[None] * field - beside


def lower_inverse(gram):
    lower = jnp.linalg.cholesky(gram)
    eye_block = jnp.eye(gram.shape[0], dtype=jnp.float32)
    return lax.linalg.triangular_solve(lower, eye_block, left_side=True, lower=True)


def general_body(vectors, levels, level_table, filter_low, filter_high):
    count_vec, rows_local, cols_local = vectors.shape
    level_ids = jnp.arange(level_table.shape[0], dtype=jnp.int32)
    onsite = jnp.sum(
        jnp.where(levels[None] == level_ids[:, None, None], level_table[:, None, None], 0.0), axis=0
    )
    center = (filter_high[0] + filter_low[0]) / 2.0
    half = (filter_high[0] - filter_low[0]) / 2.0
    first = (apply_operator(vectors, onsite) - center * vectors) / half
    filtered = 2.0 * (apply_operator(first, onsite) - center * first) / half - vectors
    total = rows_local * cols_local * lax.axis_size("lx") * lax.axis_size("ly")
    flat = filtered.reshape(count_vec, rows_local * cols_local)
    highest = lax.Precision.HIGHEST
    mine = lax.axis_index("grp")
    result = jnp.zeros_like(flat)
    for h in range(lax.axis_size("grp")):
        gram = lax.psum(jnp.dot(flat, flat.T, precision=highest), ("lx", "ly")) / total
        done = jnp.dot(lower_inverse(gram), flat, precision=highest)
        result = jnp.where(mine == h, done, result)
        shared = from_root(done, "grp", h)
        coeff = lax.psum(jnp.dot(shared, flat.T, precision=highest), ("lx", "ly")) / total
        later = mine > h
        flat = jnp.where(later, flat - jnp.dot(coeff.T, shared, precision=highest), flat)
    return result.reshape(count_vec, rows_local, cols_local)


def pair_rows(count):
    return [(i, j) for i in range(count) for j in range(i + 1)]


def lane_ids(shape):
    return lax.broadcasted_iota(jnp.int32, shape, len(shape) - 1)


def turned(tile, shift):
    shift = shift % LANE
    return pltpu.roll(tile, shift, 1) if shift else tile


def inverse_of_factor(gram, size):
    lower, inverse, recip = {}, {}, []
    for j in range(size):
        for i in range(j, size):
            value = gram[i, j]
            for k in range(j):
                value = value - lower[i, k] * lower[j, k]
            if i == j:
                recip.append(1.0 / jnp.sqrt(value))
            else:
                lower[i, j] = value * recip[j]
    for j in range(size):
        inverse[j, j] = recip[j]
        for i in range(j + 1, size):
            value = lower[i, j] * inverse[j, j]
            for k in range(j + 1, i):
                value = value + lower[i, k] * inverse[k, j]
            inverse[i, j] = -(value * recip[i])
    return inverse


def kernel(
    sizes, vec_hbm, lev_hbm, table_hbm, low_ref, high_ref, result,
    table_ref, field, level, onsite, filt, near, far, other,
    row_send, row_recv, col_send, col_recv, edge_cols, mate_rows, mate_fold, mate_cols, seam_send, seam_recv,
    parts, partial, early, grams, factors,
    load_sem, halo_send, halo_recv, grp_send, grp_recv, early_send, early_recv, gram_send, gram_recv,
):
    n_lx, n_ly = sizes
    count, rows, cols = vec_hbm.shape
    n_levels = table_hbm.shape[0]
    grp, lx, ly = lax.axis_index("grp"), lax.axis_index("lx"), lax.axis_index("ly")
    n_plane = n_lx * n_ly
    spot = lx * n_ly + ly
    me = grp * n_plane + spot
    r0, r1, c0, c1 = SUB, SUB + rows, LANE, LANE + cols
    high, wide = r1 + SUB, c1 + LANE
    split = rows // 2
    last = split // 2 // SUB * SUB
    group = 2 * SUB
    per_tile = LANE // group
    bands = rows // SUB

    def place(block, index):
        index = index % n_plane
        return (block, index // n_ly, index % n_ly)

    def remote(src, dst, send, recv, to):
        return pltpu.make_async_remote_copy(
            src_ref=src, dst_ref=dst, send_sem=send, recv_sem=recv, device_id=to, device_id_type=MESH_IDS
        )

    loads = [pltpu.make_async_copy(lev_hbm, level, load_sem.at[0])]
    loads += [pltpu.make_async_copy(table_hbm, table_ref, load_sem.at[1])]
    loads += [
        pltpu.make_async_copy(vec_hbm.at[v], field.at[v, pl.ds(r0, rows), pl.ds(c0, cols)], load_sem.at[2 + v])
        for v in range(count)
    ]
    for copy in loads[2:] + loads[:2]:
        copy.start()

    barrier = pltpu.get_barrier_semaphore()
    for d in range(1, n_plane):
        pl.semaphore_signal(barrier, inc=1, device_id=place(grp, spot + d), device_id_type=MESH_IDS)
    pl.semaphore_signal(barrier, inc=1, device_id=(1 - grp, lx, ly), device_id_type=MESH_IDS)

    @pl.when(grp == 1)
    def _():
        for d in range(1, n_plane):
            pl.semaphore_signal(barrier, inc=1, device_id=place(0, spot + d), device_id_type=MESH_IDS)

    for copy in loads[2:]:
        copy.wait()

    @pl.when(grp == 0)
    def _():
        pl.semaphore_wait(barrier, 2 * n_plane - 1)

    @pl.when(grp == 1)
    def _():
        pl.semaphore_wait(barrier, n_plane)

    partner = (1 - grp, lx, ly)
    n_link = [0]

    def across(src, dst):
        k = n_link[0]
        n_link[0] += 1
        return remote(src, dst, grp_send.at[k], grp_recv.at[k], partner)

    def band(start, stop):
        from_rows, to_rows = pl.ds(r0 + start, stop - start), pl.ds(SUB + start, stop - start)
        return across(field.at[:, from_rows, pl.ds(c0, cols)], far.at[:, to_rows, pl.ds(c0, cols)])

    sent = pl.multiple_of(r0 + (1 - grp) * split, SUB)
    nearest = across(
        field.at[:, pl.ds(sent, split), pl.ds(c0, cols)], near.at[:, pl.ds(SUB, split), pl.ds(c0, cols)]
    )
    middle = band(last - SUB, split)
    upper = band(0, last - SUB)
    packed_two = pl.ds(0, 2 * count)
    seam = across(seam_send, seam_recv)
    edges = [
        across(col_recv, mate_fold),
        across(row_recv.at[1 - grp, packed_two], mate_rows.at[1 - grp]),
    ]
    far_edge = across(row_recv.at[0, packed_two], mate_rows.at[0])

    nearest.start()
    for v in range(count):
        seam_send[2 * v:2 * v + 2, :] = jnp.where(
            grp == 0, field[v, r0 + split - 2:r0 + split, c0:c1], field[v, r0 + split:r0 + split + 2, c0:c1]
        )
    seam.start()

    for copy in loads[:2]:
        copy.wait()

    lev = level[...]
    site = jnp.zeros(lev.shape, jnp.float32)
    for k in range(n_levels):
        site = jnp.where(lev == k, table_ref[k], site)
    onsite[r0:r1, c0:c1] = site
    for v in range(count):
        row_send[0, 2 * v:2 * v + 2, :] = field[v, r1 - 2:r1, c0:c1]
        row_send[1, 2 * v:2 * v + 2, :] = field[v, r0:r0 + 2, c0:c1]
    row_send[0, 2 * count:2 * count + 1, :] = onsite[r1 - 1:r1, c0:c1]
    row_send[1, 2 * count:2 * count + 1, :] = onsite[r0:r0 + 1, c0:c1]
    lanes = lane_ids((rows, LANE))
    ends = onsite[r0:r1, c1 - LANE:c1]
    begins = onsite[r0:r1, c0:c0 + LANE]
    right = pltpu.roll(ends, LANE - 2 * count, 1)
    left = pltpu.roll(begins, 2 * count, 1)
    for v in range(count):
        here = field[v, r0:r1, c1 - LANE:c1]
        here = here if v == 0 else pltpu.roll(here, LANE - 2 * v, 1)
        right = jnp.where((lanes >= LANE - 2 - 2 * v) & (lanes < LANE - 2 * v), here, right)
        here = field[v, r0:r1, c0:c0 + LANE]
        here = here if v == 0 else pltpu.roll(here, 2 * v, 1)
        left = jnp.where((lanes >= 2 * v) & (lanes < 2 * v + 2), here, left)
    tile_lanes = lane_ids((SUB, LANE))
    for side, edge in enumerate((right, left)):
        for t in range(col_send.shape[1] // SUB):
            value = jnp.zeros((SUB, LANE), jnp.float32)
            for k in range(t * per_tile, min(bands, (t + 1) * per_tile)):
                at = group * (k - t * per_tile)
                tile = turned(edge[k * SUB:(k + 1) * SUB], at + group * (1 - side))
                value = jnp.where((tile_lanes >= at) & (tile_lanes < at + group), tile, value)
            col_send[side, t * SUB:(t + 1) * SUB] = value

    up, down = (lx + n_lx - 1) % n_lx, (lx + 1) % n_lx
    west, east = (ly + n_ly - 1) % n_ly, (ly + 1) % n_ly
    halos = []

    def halo(src, dst, x, y):
        k = len(halos)
        copy = remote(src, dst, halo_send.at[k], halo_recv.at[k], (grp, x, y))
        copy.start()
        halos.append(copy)

    for side, y in ((0, east), (1, west)):
        for slot, x in enumerate((lx, down, up)):
            halo(col_send.at[side], col_recv.at[side, slot], x, y)
    halo(row_send.at[0], row_recv.at[0], down, ly)
    halo(row_send.at[1], row_recv.at[1], up, ly)

    for copy in halos:
        copy.wait()

    for copy in edges:
        copy.start()

    @pl.when(grp == 0)
    def _():
        far_edge.start()
        middle.start()
        upper.start()

    def unfold(src, dst):
        for side in range(2):
            for k in range(bands + 2):
                slot, band_at = (1, bands - 1) if k == 0 else (2, 0) if k == bands + 1 else (0, k - 1)
                t, g = band_at // per_tile, band_at % per_tile
                tile = src[side, slot, t * SUB:(t + 1) * SUB]
                dst[side, k * SUB:(k + 1) * SUB] = turned(tile, -group * (g + 1 - side))

    def place_rows(dst, at, src):
        for v in range(count):
            dst[v, at:at + 2, c0:c1] = src[2 * v:2 * v + 2, :]

    def place_cols(dst, src, start):
        n = dst.shape[1]
        before, after = src[0, start:start + n], src[1, start:start + n]
        for v in range(count):
            dst[v, :, 0:LANE] = turned(before, 2 * v)
            dst[v, :, c1:c1 + LANE] = turned(after, -2 * v)

    unfold(col_recv, edge_cols)
    place_rows(field, r0 - 2, row_recv.at[0])
    place_rows(field, r1, row_recv.at[1])
    place_cols(field, edge_cols, 0)
    low = jnp.full((1, 1), low_ref[0], jnp.float32)
    top = jnp.full((1, 1), high_ref[0], jnp.float32)
    center = (top + low) * 0.5
    scale = 2.0 / (top - low)
    onsite[r0 - 1:r0, c0:c1] = row_recv[0, 2 * count:2 * count + 1, :]
    onsite[r1:r1 + 1, c0:c1] = row_recv[1, 2 * count:2 * count + 1, :]
    onsite[:, 0:LANE] = pltpu.roll(edge_cols[0], 2 * count, 1)
    onsite[:, c1:c1 + LANE] = pltpu.roll(edge_cols[1], LANE - 2 * count, 1)
    onsite[...] = (onsite[...] - center) * scale

    def filter_rows(src, dst, start, stop, base=0):
        at = pl.ds(start, stop - start + 2 * SUB)
        at_src = pl.ds(start - base, stop - start + 2 * SUB)
        n = stop - start + 2 * SUB
        diagonal = onsite[at, :]

        def beside(x):
            return (pltpu.roll(x, 1, 0) + pltpu.roll(x, n - 1, 0)
                    + pltpu.roll(x, 1, 1) + pltpu.roll(x, wide - 1, 1))

        for v in range(count):
            x = src[v, at_src, :]
            first = diagonal * x - beside(x) * scale
            second = 2.0 * (diagonal * first - beside(first) * scale) - x
            dst[v, start:stop] = second[SUB:SUB + stop - start, c0:c1]

    filter_rows(field, filt, 0, rows)

    pairs = pair_rows(count)
    n_self, n_cross = len(pairs), count * count
    depth = parts.shape[0]
    diag = lane_ids((depth, LANE)) == lax.broadcasted_iota(jnp.int32, (depth, LANE), 0)
    total = rows * cols * n_lx * n_ly

    def folded(a, b):
        prod = a * b
        acc = prod[:, 0:LANE]
        for k in range(1, cols // LANE):
            acc = acc + prod[:, k * LANE:(k + 1) * LANE]
        return jnp.sum(acc, axis=0, keepdims=True)

    def packed_parts():
        sums = jnp.sum(parts[...], axis=1, keepdims=True)
        return jnp.sum(jnp.where(diag, sums, 0.0), axis=0, keepdims=True)

    def spread_out(slots):
        whole = jnp.sum(slots[...], axis=0) / total
        column = jnp.sum(jnp.where(diag, whole, 0.0), axis=1, keepdims=True)
        return jnp.broadcast_to(column, (depth, LANE))

    def whole_tile(spread, p):
        return jnp.broadcast_to(spread[p:p + 1], (SUB, LANE))

    def keep_factor(gram, size):
        for (i, j), value in inverse_of_factor(gram, size).items():
            factors[i, j] = value

    parts[...] = jnp.zeros(parts.shape, jnp.float32)
    for p, (i, j) in enumerate(pairs):
        value = folded(filt[i], filt[j])
        parts[p:p + 1, :] = jnp.where(grp == 0, value, 0.0)
        q = n_self + n_cross + p
        parts[q:q + 1, :] = jnp.where(grp == 0, 0.0, value)

    def cross_parts(block_0, block_1, start, stop):
        for i in range(count):
            for j in range(count):
                p = n_self + i * count + j
                parts[p:p + 1, :] = folded(block_1[i, start:stop], block_0[j, start:stop])

    def combine(start, stop, first_row, blocks):
        for at_row in range(start, stop, SUB):
            at = pl.ds(at_row, SUB)
            for t in range(cols // LANE):
                on = pl.ds(t * LANE, LANE)
                tiles = [block[v, at, on] for block in blocks for v in range(count)]
                for i in range(count):
                    row = first_row + i
                    value = factors[row, 0] * tiles[0]
                    for j in range(1, row + 1):
                        value = value + factors[row, j] * tiles[j]
                    result[i, at, on] = value

    def place_near(start, first_rows, last_rows):
        nearest.wait_recv()
        seam.wait_recv()
        for copy in edges:
            copy.wait_recv()
        unfold(mate_fold, mate_cols)
        place_cols(near, mate_cols, start)
        place_rows(near, SUB - 2, first_rows)
        place_rows(near, SUB + split, last_rows)

    @pl.when(grp == 0)
    def _():
        partial[0] = packed_parts()
        early[spot] = partial[0]
        sends = []
        for d in range(1, n_plane):
            copy = remote(partial.at[0], early.at[spot], early_send.at[d], early_recv.at[spot], place(0, spot + d))
            copy.start()
            sends.append(copy)
        place_near(0, mate_rows.at[0], seam_recv)
        filter_rows(near, other, 0, split)
        cross_parts(filt, other, 0, split)
        partial[1] = packed_parts()
        for d in range(n_plane):
            copy = remote(partial.at[1], grams.at[me], gram_send.at[d], gram_recv.at[me], place(1, spot + d))
            copy.start()
            sends.append(copy)
        for d in range(1, n_plane):
            source = (spot + d) % n_plane
            remote(partial.at[0], early.at[source], early_send.at[d], early_recv.at[source], place(0, source)).wait_recv()
        spread = spread_out(early)
        keep_factor({(i, j): whole_tile(spread, p) for p, (i, j) in enumerate(pairs)}, count)
        combine(0, rows, 0, [filt])
        for copy in [nearest, seam, far_edge, middle, upper] + edges + sends:
            copy.wait_send()

    @pl.when(grp == 1)
    def _():
        place_near(split, seam_recv, mate_rows.at[1])
        filter_rows(near, other, split, rows, split)
        cross_parts(other, filt, split, rows)
        partial[1] = packed_parts()
        grams[me] = partial[1]
        sends = []
        for d in range(1, n_plane):
            copy = remote(partial.at[1], grams.at[me], gram_send.at[d], gram_recv.at[me], place(1, spot + d))
            copy.start()
            sends.append(copy)
        far_edge.wait_recv()
        place_cols(far, mate_cols, 0)
        place_rows(far, SUB - 2, mate_rows.at[0])
        for v in range(count):
            far[v, SUB + split:SUB + split + 2, c0:c1] = near[v, SUB:SUB + 2, c0:c1]
        middle.wait_recv()
        filter_rows(far, other, last, split)
        for d in range(1, 2 * n_plane):
            source = (me + d) % (2 * n_plane)
            remote(
                partial.at[1], grams.at[source], gram_send.at[0], gram_recv.at[source],
                place(source // n_plane, source),
            ).wait_recv()
        spread = spread_out(grams)
        gram = {}
        for p, (i, j) in enumerate(pairs):
            gram[i, j] = whole_tile(spread, p)
            q = n_self + n_cross + p
            gram[count + i, count + j] = whole_tile(spread, q)
        for i in range(count):
            for j in range(count):
                p = n_self + i * count + j
                gram[count + i, j] = whole_tile(spread, p)
        keep_factor(gram, 2 * count)
        combine(last, rows, count, [other, filt])
        upper.wait_recv()
        filter_rows(far, other, 0, last)
        combine(0, last, count, [other, filt])
        for copy in [nearest, seam] + edges + sends:
            copy.wait_send()


def fused_body(sizes, vectors, levels, level_table, filter_low, filter_high):
    count, rows, cols = vectors.shape
    n_plane = sizes[0] * sizes[1]
    high, wide = rows + 2 * SUB, cols + 2 * LANE
    depth = -(-count * (2 * count + 1) // SUB) * SUB
    packed_rows = -(-(2 * count + 1) // SUB) * SUB
    fold_rows = -(-(rows // SUB) // (LANE // (2 * SUB))) * SUB
    f32 = jnp.float32
    anywhere = pl.BlockSpec(memory_space=pl.ANY)
    in_smem = pl.BlockSpec(memory_space=pltpu.SMEM)
    dma = pltpu.SemaphoreType.DMA
    block = (count, rows, cols)
    padded, part = (count, high, wide), (count, rows // 2 + 2 * SUB, wide)
    vmem_shapes = [
        padded, None, (high, wide), block, part, part, block,
        (2, packed_rows, cols), (2, packed_rows, cols), (2, fold_rows, LANE), (2, 3, fold_rows, LANE),
        (2, high, LANE), (2, 2 * count, cols), (2, 3, fold_rows, LANE), (2, high, LANE),
        (2 * count, cols), (2 * count, cols),
        (depth, LANE), (2, 1, LANE), (n_plane, 1, LANE), (2 * n_plane, 1, LANE),
        (2 * count, 2 * count, SUB, LANE),
    ]
    scratch = [pltpu.VMEM(s, f32) if s else pltpu.VMEM((rows, cols), jnp.int32) for s in vmem_shapes]
    counts = (2 + count, 8, 8, 7, 7, n_plane, n_plane, n_plane, 2 * n_plane)
    return pl.pallas_call(
        functools.partial(kernel, sizes),
        out_shape=pltpu.VMEM(block, f32),
        in_specs=[anywhere] * 3 + [in_smem] * 2,
        out_specs=pl.BlockSpec(memory_space=pltpu.VMEM),
        scratch_shapes=[pltpu.SMEM(level_table.shape, f32)] + scratch + [dma((n,)) for n in counts],
        compiler_params=pltpu.CompilerParams(
            collective_id=0, has_side_effects=True, vmem_limit_bytes=60 * 1024 * 1024
        ),
    )(vectors, levels, level_table, filter_low, filter_high)


def solution(mesh):
    in_specs = (P("grp", "lx", "ly"), P("lx", "ly"), P(), P(), P())
    out_specs = P("grp", "lx", "ly")
    sizes = (mesh.shape["lx"], mesh.shape["ly"])

    def body(vectors, *others):
        count, rows, cols = vectors.shape
        fits = count == 4 and rows % (4 * SUB) == 0 and cols % LANE == 0
        if mesh.shape["grp"] == 2 and fits and rows >= 8 * SUB:
            return fused_body(sizes, vectors, *others)
        return general_body(vectors, *others)

    return jax.shard_map(body, mesh=mesh, in_specs=in_specs, out_specs=out_specs, check_vma=False)
```

```python
import functools

import jax
import jax.numpy as jnp
from jax import lax
from jax.experimental import pallas as pl
from jax.experimental.pallas import tpu as pltpu
from jax.sharding import PartitionSpec as P

MESH_IDS = pl.DeviceIdType.MESH
SUB, LANE = 8, 128


def padded_2(shard, sides, width):
    for axis, dim in sides:
        size, length = (lax.axis_size(axis), shard.shape[dim])
        up = [(i, (i + 1) % size) for i in range(size)]
        down = [(j, i) for i, j in up]
        last = lax.slice_in_dim(shard, length - width, length, axis=dim)
        leading = lax.slice_in_dim(shard, 0, width, axis=dim)
        before = lax.ppermute(last, axis, up)
        after = lax.ppermute(leading, axis, down)
        shard = jnp.concatenate([before, shard, after], axis=dim)
    return shard


def from_root(value, axis, source):
    kept = jnp.where(lax.axis_index(axis) == source, value, 0).astype(value.dtype)
    return lax.psum(kept, axis)


def apply_operator(field, onsite):
    padded = padded_2(field, (("lx", 1), ("ly", 2)), 1)
    beside = padded[:, 2:, 1:-1] + padded[:, :-2, 1:-1] + padded[:, 1:-1, 2:] + padded[:, 1:-1, :-2]
    return onsite[None] * field - beside


def lower_inverse(gram):
    lower = jnp.linalg.cholesky(gram)
    eye_block = jnp.eye(gram.shape[0], dtype=jnp.float32)
    return lax.linalg.triangular_solve(lower, eye_block, left_side=True, lower=True)


def general_body(vectors, levels, level_table, filter_low, filter_high):
    count_vec, rows_local, cols_local = vectors.shape
    level_ids = jnp.arange(level_table.shape[0], dtype=jnp.int32)
    onsite = jnp.sum(
        jnp.where(levels[None] == level_ids[:, None, None], level_table[:, None, None], 0.0), axis=0
    )
    center = (filter_high[0] + filter_low[0]) / 2.0
    half = (filter_high[0] - filter_low[0]) / 2.0
    first = (apply_operator(vectors, onsite) - center * vectors) / half
    filtered = 2.0 * (apply_operator(first, onsite) - center * first) / half - vectors
    total = rows_local * cols_local * lax.axis_size("lx") * lax.axis_size("ly")
    flat = filtered.reshape(count_vec, rows_local * cols_local)
    highest = lax.Precision.HIGHEST
    mine = lax.axis_index("grp")
    result = jnp.zeros_like(flat)
    for h in range(lax.axis_size("grp")):
        gram = lax.psum(jnp.dot(flat, flat.T, precision=highest), ("lx", "ly")) / total
        done = jnp.dot(lower_inverse(gram), flat, precision=highest)
        result = jnp.where(mine == h, done, result)
        shared = from_root(done, "grp", h)
        coeff = lax.psum(jnp.dot(shared, flat.T, precision=highest), ("lx", "ly")) / total
        later = mine > h
        flat = jnp.where(later, flat - jnp.dot(coeff.T, shared, precision=highest), flat)
    return result.reshape(count_vec, rows_local, cols_local)


def pair_rows(count):
    return [(i, j) for i in range(count) for j in range(i + 1)]


def lane_ids(shape):
    return lax.broadcasted_iota(jnp.int32, shape, len(shape) - 1)


def turned(tile, shift):
    shift = shift % LANE
    return pltpu.roll(tile, shift, 1) if shift else tile


def inverse_of_factor(gram, size):
    lower, inverse, recip = {}, {}, []
    for j in range(size):
        for i in range(j, size):
            value = gram[i, j]
            for k in range(j):
                value = value - lower[i, k] * lower[j, k]
            if i == j:
                recip.append(1.0 / jnp.sqrt(value))
            else:
                lower[i, j] = value * recip[j]
    for j in range(size):
        inverse[j, j] = recip[j]
        for i in range(j + 1, size):
            value = lower[i, j] * inverse[j, j]
            for k in range(j + 1, i):
                value = value + lower[i, k] * inverse[k, j]
            inverse[i, j] = -(value * recip[i])
    return inverse


def kernel(
    sizes, vec_hbm, lev_hbm, table_hbm, low_ref, high_ref, result,
    table_ref, field, level, onsite, filt, near, far, other,
    row_send, row_recv, col_send, col_recv, edge_cols, mate_rows, mate_fold, mate_cols, seam_send, seam_recv,
    parts, partial, early, grams, factors,
    load_sem, halo_send, halo_recv, grp_send, grp_recv, early_send, early_recv, gram_send, gram_recv,
):
    n_lx, n_ly = sizes
    count, rows, cols = vec_hbm.shape
    n_levels = table_hbm.shape[0]
    grp, lx, ly = lax.axis_index("grp"), lax.axis_index("lx"), lax.axis_index("ly")
    n_plane = n_lx * n_ly
    spot = lx * n_ly + ly
    me = grp * n_plane + spot
    r0, r1, c0, c1 = SUB, SUB + rows, LANE, LANE + cols
    high, wide = r1 + SUB, c1
    split = rows // 2
    last = split // 2 // SUB * SUB
    group = 2 * SUB
    per_tile = LANE // group
    bands = rows // SUB

    def place(block, index):
        index = index % n_plane
        return (block, index // n_ly, index % n_ly)

    def remote(src, dst, send, recv, to):
        return pltpu.make_async_remote_copy(
            src_ref=src, dst_ref=dst, send_sem=send, recv_sem=recv, device_id=to, device_id_type=MESH_IDS
        )

    loads = [pltpu.make_async_copy(lev_hbm, level, load_sem.at[0])]
    loads += [pltpu.make_async_copy(table_hbm, table_ref, load_sem.at[1])]
    loads += [
        pltpu.make_async_copy(vec_hbm.at[v], field.at[v, pl.ds(r0, rows), pl.ds(c0, cols)], load_sem.at[2 + v])
        for v in range(count)
    ]
    for copy in loads[2:] + loads[:2]:
        copy.start()

    barrier = pltpu.get_barrier_semaphore()
    for d in range(1, n_plane):
        pl.semaphore_signal(barrier, inc=1, device_id=place(grp, spot + d), device_id_type=MESH_IDS)
    pl.semaphore_signal(barrier, inc=1, device_id=(1 - grp, lx, ly), device_id_type=MESH_IDS)

    @pl.when(grp == 1)
    def _():
        for d in range(1, n_plane):
            pl.semaphore_signal(barrier, inc=1, device_id=place(0, spot + d), device_id_type=MESH_IDS)

    for copy in loads[2:]:
        copy.wait()

    @pl.when(grp == 0)
    def _():
        pl.semaphore_wait(barrier, 2 * n_plane - 1)

    @pl.when(grp == 1)
    def _():
        pl.semaphore_wait(barrier, n_plane)

    partner = (1 - grp, lx, ly)
    n_link = [0]

    def across(src, dst):
        k = n_link[0]
        n_link[0] += 1
        return remote(src, dst, grp_send.at[k], grp_recv.at[k], partner)

    def band(start, stop):
        from_rows, to_rows = pl.ds(r0 + start, stop - start), pl.ds(SUB + start, stop - start)
        return across(field.at[:, from_rows, pl.ds(c0, cols)], far.at[:, to_rows, pl.ds(c0, cols)])

    sent = pl.multiple_of(r0 + (1 - grp) * split, SUB)
    nearest = across(
        field.at[:, pl.ds(sent, split), pl.ds(c0, cols)], near.at[:, pl.ds(SUB, split), pl.ds(c0, cols)]
    )
    middle = band(last - SUB, split)
    upper = band(0, last - SUB)
    packed_two = pl.ds(0, 2 * count)
    seam = across(seam_send, seam_recv)
    edges = [
        across(col_recv, mate_fold),
        across(row_recv.at[1 - grp, packed_two], mate_rows.at[1 - grp]),
    ]
    far_edge = across(row_recv.at[0, packed_two], mate_rows.at[0])

    nearest.start()
    for v in range(count):
        seam_send[2 * v:2 * v + 2, :] = jnp.where(
            grp == 0, field[v, r0 + split - 2:r0 + split, c0:c1], field[v, r0 + split:r0 + split + 2, c0:c1]
        )
    seam.start()

    for copy in loads[:2]:
        copy.wait()

    lev = level[...]
    site = jnp.zeros(lev.shape, jnp.float32)
    for k in range(n_levels):
        site = jnp.where(lev == k, table_ref[k], site)
    onsite[r0:r1, c0:c1] = site
    for v in range(count):
        row_send[0, 2 * v:2 * v + 2, :] = field[v, r1 - 2:r1, c0:c1]
        row_send[1, 2 * v:2 * v + 2, :] = field[v, r0:r0 + 2, c0:c1]
    row_send[0, 2 * count:2 * count + 1, :] = onsite[r1 - 1:r1, c0:c1]
    row_send[1, 2 * count:2 * count + 1, :] = onsite[r0:r0 + 1, c0:c1]
    lanes = lane_ids((rows, LANE))
    ends = onsite[r0:r1, c1 - LANE:c1]
    begins = onsite[r0:r1, c0:c0 + LANE]
    right = pltpu.roll(ends, LANE - 2 * count, 1)
    left = pltpu.roll(begins, 2 * count, 1)
    for v in range(count):
        here = field[v, r0:r1, c1 - LANE:c1]
        here = here if v == 0 else pltpu.roll(here, LANE - 2 * v, 1)
        right = jnp.where((lanes >= LANE - 2 - 2 * v) & (lanes < LANE - 2 * v), here, right)
        here = field[v, r0:r1, c0:c0 + LANE]
        here = here if v == 0 else pltpu.roll(here, 2 * v, 1)
        left = jnp.where((lanes >= 2 * v) & (lanes < 2 * v + 2), here, left)
    tile_lanes = lane_ids((SUB, LANE))
    for side, edge in enumerate((right, left)):
        for t in range(col_send.shape[1] // SUB):
            value = jnp.zeros((SUB, LANE), jnp.float32)
            for k in range(t * per_tile, min(bands, (t + 1) * per_tile)):
                at = group * (k - t * per_tile)
                tile = turned(edge[k * SUB:(k + 1) * SUB], at + group * (1 - side))
                value = jnp.where((tile_lanes >= at) & (tile_lanes < at + group), tile, value)
            col_send[side, t * SUB:(t + 1) * SUB] = value

    up, down = (lx + n_lx - 1) % n_lx, (lx + 1) % n_lx
    west, east = (ly + n_ly - 1) % n_ly, (ly + 1) % n_ly
    halos = []

    def halo(src, dst, x, y):
        k = len(halos)
        copy = remote(src, dst, halo_send.at[k], halo_recv.at[k], (grp, x, y))
        copy.start()
        halos.append(copy)

    for side, y in ((0, east), (1, west)):
        for slot, x in enumerate((lx, down, up)):
            halo(col_send.at[side], col_recv.at[side, slot], x, y)
    halo(row_send.at[0], row_recv.at[0], down, ly)
    halo(row_send.at[1], row_recv.at[1], up, ly)

    for copy in halos:
        copy.wait()

    for copy in edges:
        copy.start()

    @pl.when(grp == 0)
    def _():
        far_edge.start()
        middle.start()
        upper.start()

    def unfold(src, dst):
        for side in range(2):
            for k in range(bands + 2):
                slot, band_at = (1, bands - 1) if k == 0 else (2, 0) if k == bands + 1 else (0, k - 1)
                t, g = band_at // per_tile, band_at % per_tile
                tile = src[side, slot, t * SUB:(t + 1) * SUB]
                dst[side, k * SUB:(k + 1) * SUB] = turned(tile, -group * (g + 1 - side))

    def place_rows(dst, at, src):
        for v in range(count):
            dst[v, at:at + 2, c0:c1] = src[2 * v:2 * v + 2, :]

    def joined(before, after):
        return jnp.where(lane_ids(before.shape) < LANE // 2, after, before)

    def place_cols(dst, src, start):
        n = dst.shape[1]
        before, after = src[0, start:start + n], src[1, start:start + n]
        for v in range(count):
            dst[v, :, 0:LANE] = joined(turned(before, 2 * v), turned(after, -2 * v))

    unfold(col_recv, edge_cols)
    place_rows(field, r0 - 2, row_recv.at[0])
    place_rows(field, r1, row_recv.at[1])
    place_cols(field, edge_cols, 0)
    low = jnp.full((1, 1), low_ref[0], jnp.float32)
    top = jnp.full((1, 1), high_ref[0], jnp.float32)
    center = (top + low) * 0.5
    scale = 2.0 / (top - low)
    onsite[r0 - 1:r0, c0:c1] = row_recv[0, 2 * count:2 * count + 1, :]
    onsite[r1:r1 + 1, c0:c1] = row_recv[1, 2 * count:2 * count + 1, :]
    onsite[:, 0:LANE] = joined(turned(edge_cols[0], 2 * count), turned(edge_cols[1], -2 * count))
    onsite[...] = (onsite[...] - center) * scale

    def filter_rows(src, dst, start, stop, base=0):
        at = pl.ds(start, stop - start + 2 * SUB)
        at_src = pl.ds(start - base, stop - start + 2 * SUB)
        n = stop - start + 2 * SUB
        diagonal = onsite[at, :]

        def beside(x):
            return (pltpu.roll(x, 1, 0) + pltpu.roll(x, n - 1, 0)
                    + pltpu.roll(x, 1, 1) + pltpu.roll(x, wide - 1, 1))

        for v in range(count):
            x = src[v, at_src, :]
            first = diagonal * x - beside(x) * scale
            second = 2.0 * (diagonal * first - beside(first) * scale) - x
            dst[v, start:stop] = second[SUB:SUB + stop - start, c0:c1]

    filter_rows(field, filt, 0, rows)

    pairs = pair_rows(count)
    n_self, n_cross = len(pairs), count * count
    depth = parts.shape[0]
    diag = lane_ids((depth, LANE)) == lax.broadcasted_iota(jnp.int32, (depth, LANE), 0)
    total = rows * cols * n_lx * n_ly

    def folded(a, b):
        prod = a * b
        acc = prod[:, 0:LANE]
        for k in range(1, cols // LANE):
            acc = acc + prod[:, k * LANE:(k + 1) * LANE]
        return jnp.sum(acc, axis=0, keepdims=True)

    def packed_parts():
        sums = jnp.sum(parts[...], axis=1, keepdims=True)
        return jnp.sum(jnp.where(diag, sums, 0.0), axis=0, keepdims=True)

    def spread_out(slots):
        whole = jnp.sum(slots[...], axis=0) / total
        column = jnp.sum(jnp.where(diag, whole, 0.0), axis=1, keepdims=True)
        return jnp.broadcast_to(column, (depth, LANE))

    def whole_tile(spread, p):
        return jnp.broadcast_to(spread[p:p + 1], (SUB, LANE))

    def keep_factor(gram, size):
        for (i, j), value in inverse_of_factor(gram, size).items():
            factors[i, j] = value

    parts[...] = jnp.zeros(parts.shape, jnp.float32)
    for p, (i, j) in enumerate(pairs):
        value = folded(filt[i], filt[j])
        parts[p:p + 1, :] = jnp.where(grp == 0, value, 0.0)
        q = n_self + n_cross + p
        parts[q:q + 1, :] = jnp.where(grp == 0, 0.0, value)

    def cross_parts(block_0, block_1, start, stop):
        for i in range(count):
            for j in range(count):
                p = n_self + i * count + j
                parts[p:p + 1, :] = folded(block_1[i, start:stop], block_0[j, start:stop])

    def combine(start, stop, first_row, blocks):
        for at_row in range(start, stop, SUB):
            at = pl.ds(at_row, SUB)
            for t in range(cols // LANE):
                on = pl.ds(t * LANE, LANE)
                tiles = [block[v, at, on] for block in blocks for v in range(count)]
                for i in range(count):
                    row = first_row + i
                    value = factors[row, 0] * tiles[0]
                    for j in range(1, row + 1):
                        value = value + factors[row, j] * tiles[j]
                    result[i, at, on] = value

    def place_near(start, first_rows, last_rows):
        seam.wait_recv()
        for copy in edges:
            copy.wait_recv()
        unfold(mate_fold, mate_cols)
        place_cols(near, mate_cols, start)
        place_rows(near, SUB - 2, first_rows)
        place_rows(near, SUB + split, last_rows)
        nearest.wait_recv()

    @pl.when(grp == 0)
    def _():
        partial[0] = packed_parts()
        early[spot] = partial[0]
        sends = []
        for d in range(1, n_plane):
            copy = remote(partial.at[0], early.at[spot], early_send.at[d], early_recv.at[spot], place(0, spot + d))
            copy.start()
            sends.append(copy)
        place_near(0, mate_rows.at[0], seam_recv)
        filter_rows(near, other, 0, split)
        cross_parts(filt, other, 0, split)
        partial[1] = packed_parts()
        for d in range(n_plane):
            copy = remote(partial.at[1], grams.at[me], gram_send.at[d], gram_recv.at[me], place(1, spot + d))
            copy.start()
            sends.append(copy)
        for d in range(1, n_plane):
            source = (spot + d) % n_plane
            remote(partial.at[0], early.at[source], early_send.at[d], early_recv.at[source], place(0, source)).wait_recv()
        spread = spread_out(early)
        keep_factor({(i, j): whole_tile(spread, p) for p, (i, j) in enumerate(pairs)}, count)
        combine(0, rows, 0, [filt])
        for copy in [nearest, seam, far_edge, middle, upper] + edges + sends:
            copy.wait_send()

    @pl.when(grp == 1)
    def _():
        place_near(split, seam_recv, mate_rows.at[1])
        filter_rows(near, other, split, rows, split)
        cross_parts(other, filt, split, rows)
        partial[1] = packed_parts()
        grams[me] = partial[1]
        sends = []
        for d in range(1, n_plane):
            copy = remote(partial.at[1], grams.at[me], gram_send.at[d], gram_recv.at[me], place(1, spot + d))
            copy.start()
            sends.append(copy)
        far_edge.wait_recv()
        place_cols(far, mate_cols, 0)
        place_rows(far, SUB - 2, mate_rows.at[0])
        for v in range(count):
            far[v, SUB + split:SUB + split + 2, c0:c1] = near[v, SUB:SUB + 2, c0:c1]
        middle.wait_recv()
        filter_rows(far, other, last, split)
        for copy in [nearest, seam] + edges + sends:
            copy.wait_send()
        for d in range(1, 2 * n_plane):
            source = (me + d) % (2 * n_plane)
            remote(
                partial.at[1], grams.at[source], gram_send.at[0], gram_recv.at[source],
                place(source // n_plane, source),
            ).wait_recv()
        spread = spread_out(grams)
        gram = {}
        for p, (i, j) in enumerate(pairs):
            gram[i, j] = whole_tile(spread, p)
            q = n_self + n_cross + p
            gram[count + i, count + j] = whole_tile(spread, q)
        for i in range(count):
            for j in range(count):
                p = n_self + i * count + j
                gram[count + i, j] = whole_tile(spread, p)
        keep_factor(gram, 2 * count)
        combine(last, rows, count, [other, filt])
        upper.wait_recv()
        filter_rows(far, other, 0, last)
        combine(0, last, count, [other, filt])


def fused_body(sizes, vectors, levels, level_table, filter_low, filter_high):
    count, rows, cols = vectors.shape
    n_plane = sizes[0] * sizes[1]
    high, wide = rows + 2 * SUB, cols + LANE
    depth = -(-count * (2 * count + 1) // SUB) * SUB
    packed_rows = -(-(2 * count + 1) // SUB) * SUB
    fold_rows = -(-(rows // SUB) // (LANE // (2 * SUB))) * SUB
    f32 = jnp.float32
    anywhere = pl.BlockSpec(memory_space=pl.ANY)
    in_smem = pl.BlockSpec(memory_space=pltpu.SMEM)
    dma = pltpu.SemaphoreType.DMA
    block = (count, rows, cols)
    padded, part = (count, high, wide), (count, rows // 2 + 2 * SUB, wide)
    vmem_shapes = [
        padded, None, (high, wide), block, part, part, block,
        (2, packed_rows, cols), (2, packed_rows, cols), (2, fold_rows, LANE), (2, 3, fold_rows, LANE),
        (2, high, LANE), (2, 2 * count, cols), (2, 3, fold_rows, LANE), (2, high, LANE),
        (2 * count, cols), (2 * count, cols),
        (depth, LANE), (2, 1, LANE), (n_plane, 1, LANE), (2 * n_plane, 1, LANE),
        (2 * count, 2 * count, SUB, LANE),
    ]
    scratch = [pltpu.VMEM(s, f32) if s else pltpu.VMEM((rows, cols), jnp.int32) for s in vmem_shapes]
    counts = (2 + count, 8, 8, 7, 7, n_plane, n_plane, n_plane, 2 * n_plane)
    return pl.pallas_call(
        functools.partial(kernel, sizes),
        out_shape=pltpu.VMEM(block, f32),
        in_specs=[anywhere] * 3 + [in_smem] * 2,
        out_specs=pl.BlockSpec(memory_space=pltpu.VMEM),
        scratch_shapes=[pltpu.SMEM(level_table.shape, f32)] + scratch + [dma((n,)) for n in counts],
        compiler_params=pltpu.CompilerParams(
            collective_id=0, has_side_effects=True, vmem_limit_bytes=60 * 1024 * 1024
        ),
    )(vectors, levels, level_table, filter_low, filter_high)


def solution(mesh):
    in_specs = (P("grp", "lx", "ly"), P("lx", "ly"), P(), P(), P())
    out_specs = P("grp", "lx", "ly")
    sizes = (mesh.shape["lx"], mesh.shape["ly"])

    def body(vectors, *others):
        count, rows, cols = vectors.shape
        fits = count == 4 and rows % (4 * SUB) == 0 and cols % LANE == 0
        if mesh.shape["grp"] == 2 and fits and rows >= 8 * SUB:
            return fused_body(sizes, vectors, *others)
        return general_body(vectors, *others)

    return jax.shard_map(body, mesh=mesh, in_specs=in_specs, out_specs=out_specs, check_vma=False)
```

```python
import functools

import jax
import jax.numpy as jnp
from jax import lax
from jax.experimental import pallas as pl
from jax.experimental.pallas import tpu as pltpu
from jax.sharding import PartitionSpec as P

MESH_IDS = pl.DeviceIdType.MESH
SUB, LANE = 8, 128


def padded_2(shard, sides, width):
    for axis, dim in sides:
        size, length = (lax.axis_size(axis), shard.shape[dim])
        up = [(i, (i + 1) % size) for i in range(size)]
        down = [(j, i) for i, j in up]
        last = lax.slice_in_dim(shard, length - width, length, axis=dim)
        leading = lax.slice_in_dim(shard, 0, width, axis=dim)
        before = lax.ppermute(last, axis, up)
        after = lax.ppermute(leading, axis, down)
        shard = jnp.concatenate([before, shard, after], axis=dim)
    return shard


def from_root(value, axis, source):
    kept = jnp.where(lax.axis_index(axis) == source, value, 0).astype(value.dtype)
    return lax.psum(kept, axis)


def apply_operator(field, onsite):
    padded = padded_2(field, (("lx", 1), ("ly", 2)), 1)
    beside = padded[:, 2:, 1:-1] + padded[:, :-2, 1:-1] + padded[:, 1:-1, 2:] + padded[:, 1:-1, :-2]
    return onsite[None] * field - beside


def lower_inverse(gram):
    lower = jnp.linalg.cholesky(gram)
    eye_block = jnp.eye(gram.shape[0], dtype=jnp.float32)
    return lax.linalg.triangular_solve(lower, eye_block, left_side=True, lower=True)


def general_body(vectors, levels, level_table, filter_low, filter_high):
    count_vec, rows_local, cols_local = vectors.shape
    level_ids = jnp.arange(level_table.shape[0], dtype=jnp.int32)
    onsite = jnp.sum(
        jnp.where(levels[None] == level_ids[:, None, None], level_table[:, None, None], 0.0), axis=0
    )
    center = (filter_high[0] + filter_low[0]) / 2.0
    half = (filter_high[0] - filter_low[0]) / 2.0
    first = (apply_operator(vectors, onsite) - center * vectors) / half
    filtered = 2.0 * (apply_operator(first, onsite) - center * first) / half - vectors
    total = rows_local * cols_local * lax.axis_size("lx") * lax.axis_size("ly")
    flat = filtered.reshape(count_vec, rows_local * cols_local)
    highest = lax.Precision.HIGHEST
    mine = lax.axis_index("grp")
    result = jnp.zeros_like(flat)
    for h in range(lax.axis_size("grp")):
        gram = lax.psum(jnp.dot(flat, flat.T, precision=highest), ("lx", "ly")) / total
        done = jnp.dot(lower_inverse(gram), flat, precision=highest)
        result = jnp.where(mine == h, done, result)
        shared = from_root(done, "grp", h)
        coeff = lax.psum(jnp.dot(shared, flat.T, precision=highest), ("lx", "ly")) / total
        later = mine > h
        flat = jnp.where(later, flat - jnp.dot(coeff.T, shared, precision=highest), flat)
    return result.reshape(count_vec, rows_local, cols_local)


def pair_rows(count):
    return [(i, j) for i in range(count) for j in range(i + 1)]


def lane_ids(shape):
    return lax.broadcasted_iota(jnp.int32, shape, len(shape) - 1)


def turned(tile, shift):
    shift = shift % LANE
    return pltpu.roll(tile, shift, 1) if shift else tile


def inverse_of_factor(gram, size):
    lower, inverse, recip = {}, {}, []
    for j in range(size):
        for i in range(j, size):
            value = gram[i, j]
            for k in range(j):
                value = value - lower[i, k] * lower[j, k]
            if i == j:
                recip.append(1.0 / jnp.sqrt(value))
            else:
                lower[i, j] = value * recip[j]
    for j in range(size):
        inverse[j, j] = recip[j]
        for i in range(j + 1, size):
            value = lower[i, j] * inverse[j, j]
            for k in range(j + 1, i):
                value = value + lower[i, k] * inverse[k, j]
            inverse[i, j] = -(value * recip[i])
    return inverse


def kernel(
    sizes, vec_hbm, lev_hbm, table_hbm, low_ref, high_ref, result,
    table_ref, field, level, onsite, filt, near, far, other,
    row_send, row_recv, col_send, col_recv, edge_cols, mate_rows, mate_fold, mate_cols, seam_send, seam_recv,
    parts, partial, early, grams, factors,
    load_sem, halo_send, halo_recv, grp_send, grp_recv, early_send, early_recv, gram_send, gram_recv,
):
    n_lx, n_ly = sizes
    count, rows, cols = vec_hbm.shape
    n_levels = table_hbm.shape[0]
    grp, lx, ly = lax.axis_index("grp"), lax.axis_index("lx"), lax.axis_index("ly")
    n_plane = n_lx * n_ly
    spot = lx * n_ly + ly
    me = grp * n_plane + spot
    r0, r1, c0, c1 = SUB, SUB + rows, LANE, LANE + cols
    high, wide = r1 + SUB, c1
    split = rows // 2
    last = split // 2 // SUB * SUB
    group = 2 * SUB
    per_tile = LANE // group
    bands = rows // SUB

    def place(block, index):
        index = index % n_plane
        return (block, index // n_ly, index % n_ly)

    def remote(src, dst, send, recv, to):
        return pltpu.make_async_remote_copy(
            src_ref=src, dst_ref=dst, send_sem=send, recv_sem=recv, device_id=to, device_id_type=MESH_IDS
        )

    loads = [pltpu.make_async_copy(lev_hbm, level, load_sem.at[0])]
    loads += [pltpu.make_async_copy(table_hbm, table_ref, load_sem.at[1])]
    loads += [
        pltpu.make_async_copy(vec_hbm.at[v], field.at[v, pl.ds(r0, rows), pl.ds(c0, cols)], load_sem.at[2 + v])
        for v in range(count)
    ]
    for copy in loads[2:] + loads[:2]:
        copy.start()

    barrier = pltpu.get_barrier_semaphore()
    for d in range(1, n_plane):
        pl.semaphore_signal(barrier, inc=1, device_id=place(grp, spot + d), device_id_type=MESH_IDS)
    pl.semaphore_signal(barrier, inc=1, device_id=(1 - grp, lx, ly), device_id_type=MESH_IDS)

    @pl.when(grp == 1)
    def _():
        for d in range(1, n_plane):
            pl.semaphore_signal(barrier, inc=1, device_id=place(0, spot + d), device_id_type=MESH_IDS)

    for copy in loads[2:]:
        copy.wait()

    @pl.when(grp == 0)
    def _():
        pl.semaphore_wait(barrier, 2 * n_plane - 1)

    @pl.when(grp == 1)
    def _():
        pl.semaphore_wait(barrier, n_plane)

    partner = (1 - grp, lx, ly)
    n_link = [0]

    def across(src, dst):
        k = n_link[0]
        n_link[0] += 1
        return remote(src, dst, grp_send.at[k], grp_recv.at[k], partner)

    def band(start, stop):
        from_rows, to_rows = pl.ds(r0 + start, stop - start), pl.ds(SUB + start, stop - start)
        return across(field.at[:, from_rows, pl.ds(c0, cols)], far.at[:, to_rows, pl.ds(c0, cols)])

    sent = pl.multiple_of(r0 + (1 - grp) * split, SUB)
    nearest = across(
        field.at[:, pl.ds(sent, split), pl.ds(c0, cols)], near.at[:, pl.ds(SUB, split), pl.ds(c0, cols)]
    )
    middle = band(last - SUB, split)
    upper = band(0, last - SUB)
    packed_two = pl.ds(0, 2 * count)
    seam = across(seam_send, seam_recv)
    edges = [
        across(col_recv, mate_fold),
        across(row_recv.at[1 - grp, packed_two], mate_rows.at[1 - grp]),
    ]
    far_edge = across(row_recv.at[0, packed_two], mate_rows.at[0])

    nearest.start()
    for v in range(count):
        seam_send[2 * v:2 * v + 2, :] = jnp.where(
            grp == 0, field[v, r0 + split - 2:r0 + split, c0:c1], field[v, r0 + split:r0 + split + 2, c0:c1]
        )
    seam.start()

    for copy in loads[:2]:
        copy.wait()

    lev = level[...]
    site = jnp.zeros(lev.shape, jnp.float32)
    for k in range(n_levels):
        site = jnp.where(lev == k, table_ref[k], site)
    onsite[r0:r1, c0:c1] = site
    for v in range(count):
        row_send[0, 2 * v:2 * v + 2, :] = field[v, r1 - 2:r1, c0:c1]
        row_send[1, 2 * v:2 * v + 2, :] = field[v, r0:r0 + 2, c0:c1]
    row_send[0, 2 * count:2 * count + 1, :] = onsite[r1 - 1:r1, c0:c1]
    row_send[1, 2 * count:2 * count + 1, :] = onsite[r0:r0 + 1, c0:c1]
    lanes = lane_ids((rows, LANE))
    ends = onsite[r0:r1, c1 - LANE:c1]
    begins = onsite[r0:r1, c0:c0 + LANE]
    right = pltpu.roll(ends, LANE - 2 * count, 1)
    left = pltpu.roll(begins, 2 * count, 1)
    for v in range(count):
        here = field[v, r0:r1, c1 - LANE:c1]
        here = here if v == 0 else pltpu.roll(here, LANE - 2 * v, 1)
        right = jnp.where((lanes >= LANE - 2 - 2 * v) & (lanes < LANE - 2 * v), here, right)
        here = field[v, r0:r1, c0:c0 + LANE]
        here = here if v == 0 else pltpu.roll(here, 2 * v, 1)
        left = jnp.where((lanes >= 2 * v) & (lanes < 2 * v + 2), here, left)
    tile_lanes = lane_ids((SUB, LANE))
    for side, edge in enumerate((right, left)):
        for t in range(col_send.shape[1] // SUB):
            value = jnp.zeros((SUB, LANE), jnp.float32)
            for k in range(t * per_tile, min(bands, (t + 1) * per_tile)):
                at = group * (k - t * per_tile)
                tile = turned(edge[k * SUB:(k + 1) * SUB], at + group * (1 - side))
                value = jnp.where((tile_lanes >= at) & (tile_lanes < at + group), tile, value)
            col_send[side, t * SUB:(t + 1) * SUB] = value

    up, down = (lx + n_lx - 1) % n_lx, (lx + 1) % n_lx
    west, east = (ly + n_ly - 1) % n_ly, (ly + 1) % n_ly
    halos = []

    def halo(src, dst, x, y):
        k = len(halos)
        copy = remote(src, dst, halo_send.at[k], halo_recv.at[k], (grp, x, y))
        copy.start()
        halos.append(copy)

    for side, y in ((0, east), (1, west)):
        for slot, x in enumerate((lx, down, up)):
            halo(col_send.at[side], col_recv.at[side, slot], x, y)
    halo(row_send.at[0], row_recv.at[0], down, ly)
    halo(row_send.at[1], row_recv.at[1], up, ly)

    for copy in halos:
        copy.wait()

    for copy in edges:
        copy.start()

    @pl.when(grp == 0)
    def _():
        far_edge.start()
        middle.start()

    def unfold(src, dst):
        for side in range(2):
            for k in range(bands + 2):
                slot, band_at = (1, bands - 1) if k == 0 else (2, 0) if k == bands + 1 else (0, k - 1)
                t, g = band_at // per_tile, band_at % per_tile
                tile = src[side, slot, t * SUB:(t + 1) * SUB]
                dst[side, k * SUB:(k + 1) * SUB] = turned(tile, -group * (g + 1 - side))

    def place_rows(dst, at, src):
        for v in range(count):
            dst[v, at:at + 2, c0:c1] = src[2 * v:2 * v + 2, :]

    def joined(before, after):
        return jnp.where(lane_ids(before.shape) < LANE // 2, after, before)

    def place_cols(dst, src, start):
        n = dst.shape[1]
        before, after = src[0, start:start + n], src[1, start:start + n]
        for v in range(count):
            dst[v, :, 0:LANE] = joined(turned(before, 2 * v), turned(after, -2 * v))

    unfold(col_recv, edge_cols)
    place_rows(field, r0 - 2, row_recv.at[0])
    place_rows(field, r1, row_recv.at[1])
    place_cols(field, edge_cols, 0)
    low = jnp.full((1, 1), low_ref[0], jnp.float32)
    top = jnp.full((1, 1), high_ref[0], jnp.float32)
    center = (top + low) * 0.5
    scale = 2.0 / (top - low)
    onsite[r0 - 1:r0, c0:c1] = row_recv[0, 2 * count:2 * count + 1, :]
    onsite[r1:r1 + 1, c0:c1] = row_recv[1, 2 * count:2 * count + 1, :]
    onsite[:, 0:LANE] = joined(turned(edge_cols[0], 2 * count), turned(edge_cols[1], -2 * count))
    onsite[...] = (onsite[...] - center) * scale

    def filter_rows(src, dst, start, stop, base=0):
        at = pl.ds(start, stop - start + 2 * SUB)
        at_src = pl.ds(start - base, stop - start + 2 * SUB)
        n = stop - start + 2 * SUB
        diagonal = onsite[at, :]

        def beside(x):
            return (pltpu.roll(x, 1, 0) + pltpu.roll(x, n - 1, 0)
                    + pltpu.roll(x, 1, 1) + pltpu.roll(x, wide - 1, 1))

        for v in range(count):
            x = src[v, at_src, :]
            first = diagonal * x - beside(x) * scale
            second = 2.0 * (diagonal * first - beside(first) * scale) - x
            dst[v, start:stop] = second[SUB:SUB + stop - start, c0:c1]

    filter_rows(field, filt, 0, rows)

    pairs = pair_rows(count)
    n_self, n_cross = len(pairs), count * count
    depth = parts.shape[0]
    diag = lane_ids((depth, LANE)) == lax.broadcasted_iota(jnp.int32, (depth, LANE), 0)
    total = rows * cols * n_lx * n_ly

    def folded(a, b):
        prod = a * b
        acc = prod[:, 0:LANE]
        for k in range(1, cols // LANE):
            acc = acc + prod[:, k * LANE:(k + 1) * LANE]
        return jnp.sum(acc, axis=0, keepdims=True)

    def packed_parts():
        sums = jnp.sum(parts[...], axis=1, keepdims=True)
        return jnp.sum(jnp.where(diag, sums, 0.0), axis=0, keepdims=True)

    def spread_out(slots):
        whole = jnp.sum(slots[...], axis=0) / total
        column = jnp.sum(jnp.where(diag, whole, 0.0), axis=1, keepdims=True)
        return jnp.broadcast_to(column, (depth, LANE))

    def whole_tile(spread, p):
        return jnp.broadcast_to(spread[p:p + 1], (SUB, LANE))

    def keep_factor(gram, size):
        for (i, j), value in inverse_of_factor(gram, size).items():
            factors[i, j] = value

    parts[...] = jnp.zeros(parts.shape, jnp.float32)
    for p, (i, j) in enumerate(pairs):
        value = folded(filt[i], filt[j])
        parts[p:p + 1, :] = jnp.where(grp == 0, value, 0.0)
        q = n_self + n_cross + p
        parts[q:q + 1, :] = jnp.where(grp == 0, 0.0, value)

    def cross_parts(block_0, block_1, start, stop):
        for i in range(count):
            for j in range(count):
                p = n_self + i * count + j
                parts[p:p + 1, :] = folded(block_1[i, start:stop], block_0[j, start:stop])

    def combine(start, stop, first_row, blocks):
        for at_row in range(start, stop, SUB):
            at = pl.ds(at_row, SUB)
            for t in range(cols // LANE):
                on = pl.ds(t * LANE, LANE)
                tiles = [block[v, at, on] for block in blocks for v in range(count)]
                for i in range(count):
                    row = first_row + i
                    value = factors[row, 0] * tiles[0]
                    for j in range(1, row + 1):
                        value = value + factors[row, j] * tiles[j]
                    result[i, at, on] = value

    def place_near(start, first_rows, last_rows):
        seam.wait_recv()
        for copy in edges:
            copy.wait_recv()
        unfold(mate_fold, mate_cols)
        place_cols(near, mate_cols, start)
        place_rows(near, SUB - 2, first_rows)
        place_rows(near, SUB + split, last_rows)
        nearest.wait_recv()

    @pl.when(grp == 0)
    def _():
        partial[0] = packed_parts()
        early[spot] = partial[0]
        sends = []
        for d in range(1, n_plane):
            copy = remote(partial.at[0], early.at[spot], early_send.at[d], early_recv.at[spot], place(0, spot + d))
            copy.start()
            sends.append(copy)
        place_near(0, mate_rows.at[0], seam_recv)
        filter_rows(near, other, 0, split)
        cross_parts(filt, other, 0, split)
        partial[1] = packed_parts()
        for d in range(n_plane):
            copy = remote(partial.at[1], grams.at[me], gram_send.at[d], gram_recv.at[me], place(1, spot + d))
            copy.start()
            sends.append(copy)
        upper.start()
        for d in range(1, n_plane):
            source = (spot + d) % n_plane
            remote(partial.at[0], early.at[source], early_send.at[d], early_recv.at[source], place(0, source)).wait_recv()
        spread = spread_out(early)
        keep_factor({(i, j): whole_tile(spread, p) for p, (i, j) in enumerate(pairs)}, count)
        combine(0, rows, 0, [filt])
        for copy in [nearest, seam, far_edge, middle, upper] + edges + sends:
            copy.wait_send()

    @pl.when(grp == 1)
    def _():
        place_near(split, seam_recv, mate_rows.at[1])
        filter_rows(near, other, split, rows, split)
        cross_parts(other, filt, split, rows)
        partial[1] = packed_parts()
        grams[me] = partial[1]
        sends = []
        for d in range(1, n_plane):
            copy = remote(partial.at[1], grams.at[me], gram_send.at[d], gram_recv.at[me], place(1, spot + d))
            copy.start()
            sends.append(copy)
        far_edge.wait_recv()
        place_cols(far, mate_cols, 0)
        place_rows(far, SUB - 2, mate_rows.at[0])
        for v in range(count):
            far[v, SUB + split:SUB + split + 2, c0:c1] = near[v, SUB:SUB + 2, c0:c1]
        middle.wait_recv()
        filter_rows(far, other, last, split)
        for copy in [nearest, seam] + edges + sends:
            copy.wait_send()
        for d in range(1, 2 * n_plane):
            source = (me + d) % (2 * n_plane)
            remote(
                partial.at[1], grams.at[source], gram_send.at[0], gram_recv.at[source],
                place(source // n_plane, source),
            ).wait_recv()
        spread = spread_out(grams)
        gram = {}
        for p, (i, j) in enumerate(pairs):
            gram[i, j] = whole_tile(spread, p)
            q = n_self + n_cross + p
            gram[count + i, count + j] = whole_tile(spread, q)
        for i in range(count):
            for j in range(count):
                p = n_self + i * count + j
                gram[count + i, j] = whole_tile(spread, p)
        keep_factor(gram, 2 * count)
        combine(last, rows, count, [other, filt])
        upper.wait_recv()
        filter_rows(far, other, 0, last)
        combine(0, last, count, [other, filt])


def fused_body(sizes, vectors, levels, level_table, filter_low, filter_high):
    count, rows, cols = vectors.shape
    n_plane = sizes[0] * sizes[1]
    high, wide = rows + 2 * SUB, cols + LANE
    depth = -(-count * (2 * count + 1) // SUB) * SUB
    packed_rows = -(-(2 * count + 1) // SUB) * SUB
    fold_rows = -(-(rows // SUB) // (LANE // (2 * SUB))) * SUB
    f32 = jnp.float32
    anywhere = pl.BlockSpec(memory_space=pl.ANY)
    in_smem = pl.BlockSpec(memory_space=pltpu.SMEM)
    dma = pltpu.SemaphoreType.DMA
    block = (count, rows, cols)
    padded, part = (count, high, wide), (count, rows // 2 + 2 * SUB, wide)
    vmem_shapes = [
        padded, None, (high, wide), block, part, part, block,
        (2, packed_rows, cols), (2, packed_rows, cols), (2, fold_rows, LANE), (2, 3, fold_rows, LANE),
        (2, high, LANE), (2, 2 * count, cols), (2, 3, fold_rows, LANE), (2, high, LANE),
        (2 * count, cols), (2 * count, cols),
        (depth, LANE), (2, 1, LANE), (n_plane, 1, LANE), (2 * n_plane, 1, LANE),
        (2 * count, 2 * count, SUB, LANE),
    ]
    scratch = [pltpu.VMEM(s, f32) if s else pltpu.VMEM((rows, cols), jnp.int32) for s in vmem_shapes]
    counts = (2 + count, 8, 8, 7, 7, n_plane, n_plane, n_plane, 2 * n_plane)
    return pl.pallas_call(
        functools.partial(kernel, sizes),
        out_shape=pltpu.VMEM(block, f32),
        in_specs=[anywhere] * 3 + [in_smem] * 2,
        out_specs=pl.BlockSpec(memory_space=pltpu.VMEM),
        scratch_shapes=[pltpu.SMEM(level_table.shape, f32)] + scratch + [dma((n,)) for n in counts],
        compiler_params=pltpu.CompilerParams(
            collective_id=0, has_side_effects=True, vmem_limit_bytes=60 * 1024 * 1024
        ),
    )(vectors, levels, level_table, filter_low, filter_high)


def solution(mesh):
    in_specs = (P("grp", "lx", "ly"), P("lx", "ly"), P(), P(), P())
    out_specs = P("grp", "lx", "ly")
    sizes = (mesh.shape["lx"], mesh.shape["ly"])

    def body(vectors, *others):
        count, rows, cols = vectors.shape
        fits = count == 4 and rows % (4 * SUB) == 0 and cols % LANE == 0
        if mesh.shape["grp"] == 2 and fits and rows >= 8 * SUB:
            return fused_body(sizes, vectors, *others)
        return general_body(vectors, *others)

    return jax.shard_map(body, mesh=mesh, in_specs=in_specs, out_specs=out_specs, check_vma=False)
```
